32 devices in a mesh: grp: 2 (over y), param: 4 (over z), ex: 4 (over x, core).
Axes of the slice: x: 2, y: 2, z: 4, core: 2. Of those that a mesh axis runs over, the one named last changes fastest.
Arguments:
- activations: bfloat16 [8, 256, 4096], P(('grp', 'ex'), None, 'param'), parts along dimension 0, may hold values from -96 to 96
- backprops: bfloat16 [8, 256, 4096], P(('grp', 'ex'), None, 'param'), parts along dimension 0, may hold values from -96 to 96
- block_counters: int32 [2, 4], P(None, 'param'), may hold values from 0 to 999999
Outputs:
- features: float32 [8, 2048], P(('grp', 'ex'), 'param'), parts along dimension 0
- grad_norm: float32 [8], P(('grp', 'ex')), parts along dimension 0
The draws below stay inside these ranges and needn't reach their ends.
There are 2 independent parts, one for each index of `grp`. The reference program is written for one: setup_inputs(seed, part) draws one part's arguments, and reference() takes and returns one part's arrays. A program takes and returns all parts, laid end to end along the dimension named above; an argument that names none is the same for every part. Nothing has to cross between parts.
All inputs are finite; a program needn't handle non-finite values.
Results may differ from the reference program's by a relative error of at most 0.006.
Values may be sent and summed in bfloat16 or wider, within the bound.
No kernel may reach another device: no remote copies, remote signals or barrier semaphores. Data moves between devices by JAX's collectives and lax.ppermute only.
A program may use at most 64 MiB of HBM per device.

```python
import math
import jax
import jax.numpy as jnp
from jax import lax

D = 4096
K = 2048
SEQ = 256
EXAMPLES = 4
ROW_BLOCK = 1024
N_PARAM = 4


def scaled_features(key, salt):
    folded = jax.random.fold_in(key, salt)
    noise_key, column_key, token_key = jax.random.split(folded, 3)
    column_ramp = jnp.sqrt(1.0 + 2.0 * jnp.arange(D, dtype=jnp.float32) / D)
    randomness = jnp.clip(jax.random.normal(noise_key, (EXAMPLES, SEQ, D), jnp.float32), -5.0, 5.0)
    column_top = 10.0
    column_scale = jnp.exp(jax.random.uniform(column_key, (D,), jnp.float32) * math.log(column_top)) * column_ramp
    token_scale = jnp.exp(jax.random.uniform(token_key, (EXAMPLES, SEQ, 1), jnp.float32) * math.log(3.0))
    return jnp.clip(randomness * column_scale * token_scale, -96.0, 96.0).astype(jnp.bfloat16)


def draw_activations(key, part):
    return scaled_features(key, 11)


def draw_backprops(key, part):
    return scaled_features(key, 23)


def set_ends(entries, stream_key, least, top_value):
    shape = entries.shape
    index_at = [jax.random.randint(jax.random.fold_in(stream_key, axis), (), 0, shape[axis]) for axis in range(len(shape))]
    entries = entries.at[tuple(index_at)].set(least)
    longest = shape.index(max(shape))
    index_at[longest] = (index_at[longest] + 1) % shape[longest]
    return entries.at[tuple(index_at)].set(top_value)


def setup_inputs(seed: int = 0, part: int = 0) -> dict:
    seeds = jax.random.split(jax.random.key(seed), 4)
    part_keys = jax.random.split(jax.random.fold_in(seeds[3], part), 4)
    activations = draw_activations(jax.random.fold_in(jax.random.fold_in(seeds[3], part), 71), part)
    backprops = draw_backprops(jax.random.fold_in(jax.random.fold_in(seeds[3], part), 71), part)
    block_counters = set_ends(jax.random.randint(seeds[2], (2, N_PARAM), 0, 1000000), jax.random.fold_in(seeds[2], 1), 0, 999999).astype(jnp.int32)
    return {"activations": activations, "backprops": backprops, "block_counters": block_counters}


mix_factor = 73244475
epsilon = 1e-06

def scramble(hashed):
    hashed = jnp.bitwise_xor(hashed, lax.shift_right_logical(hashed, jnp.int32(16)))
    hashed = hashed * mix_factor
    hashed = jnp.bitwise_xor(hashed, lax.shift_right_logical(hashed, jnp.int32(16)))
    hashed = hashed * mix_factor
    return jnp.bitwise_xor(hashed, lax.shift_right_logical(hashed, jnp.int32(16)))

def gaussian_block(stream, row_ids, col_ids):
    hashed = stream * 668265261 + row_ids[:, None] * 374761393 + col_ids[None, :] * 1103515245
    hashed = scramble(hashed)
    total_bytes = jnp.bitwise_and(hashed, 255)
    for shift_bits in (8, 16, 24):
        total_bytes = total_bytes + jnp.bitwise_and(lax.shift_right_logical(hashed, jnp.int32(shift_bits)), 255)
    return ((total_bytes - 510).astype(jnp.float32) * (1.0 / 128.0)).astype(jnp.bfloat16)

def reference(activations, backprops, block_counters):
    proj_cols = jnp.arange(K, dtype=jnp.int32)
    all_cols = jnp.arange(D, dtype=jnp.int32)
    acts_wide = activations.astype(jnp.float32)
    backs_wide = backprops.astype(jnp.float32)

    def per_block(block):
        first_row = (block * ROW_BLOCK).astype(jnp.int32)
        row_ids = first_row + jnp.arange(ROW_BLOCK, dtype=jnp.int32)
        row_proj = gaussian_block(block_counters[0, block], row_ids, proj_cols).astype(jnp.float32)
        col_proj = gaussian_block(block_counters[1, block], all_cols, proj_cols).astype(jnp.float32)
        acts_rows = lax.dynamic_slice_in_dim(acts_wide, first_row, ROW_BLOCK, 2)
        grad = jnp.einsum('etr,etd->erd', acts_rows, backs_wide).astype(jnp.bfloat16)
        grad_wide = grad.astype(jnp.float32)
        squares = lax.optimization_barrier(jnp.sum(grad_wide * grad_wide, axis=(1, 2)))
        mixed = jnp.einsum('erd,dk->erk', grad_wide, col_proj)
        partial_sum = lax.optimization_barrier(jnp.sum(mixed * row_proj[None], axis=1))
        return (partial_sum, squares)
    partials, square_parts = lax.map(per_block, jnp.arange(N_PARAM, dtype=jnp.int32))
    projected = lax.optimization_barrier(jnp.sum(partials, axis=0))
    sumsq = lax.optimization_barrier(jnp.sum(square_parts, axis=0))
    features = projected * lax.rsqrt(sumsq + epsilon)[:, None]
    return (features, jnp.sqrt(sumsq))
```

```python
import functools

import jax
import jax.numpy as jnp
from jax import lax
from jax.experimental import pallas as pl
from jax.experimental.pallas import tpu as pltpu
from jax.sharding import PartitionSpec as P

K = 2048

mix_factor = 73244475
stream_factor = 668265261
row_factor = 374761393
col_factor = 1103515245
epsilon = 1e-06
unscale = 1.0 / (128.0 * 128.0)

tile = 256
sub_rows = 16
sub_cols = 256


def wrapped(number):
    return jnp.int32((number + 2**31) % 2**32 - 2**31)


def scramble(hashed):
    sixteen = jnp.int32(16)
    hashed = jnp.bitwise_xor(hashed, lax.shift_right_logical(hashed, sixteen))
    hashed = hashed * mix_factor
    hashed = jnp.bitwise_xor(hashed, lax.shift_right_logical(hashed, sixteen))
    hashed = hashed * mix_factor
    return jnp.bitwise_xor(hashed, lax.shift_right_logical(hashed, sixteen))


def to_gauss(hashed):
    hashed = scramble(hashed)
    pairs = jnp.int32(0x00FF00FF)
    two_sums = jnp.bitwise_and(hashed, pairs) + jnp.bitwise_and(
        lax.shift_right_logical(hashed, jnp.int32(8)), pairs
    )
    total = lax.shift_right_logical(two_sums * jnp.int32(0x10001), jnp.int32(16))
    return (total - 510).astype(jnp.float32).astype(jnp.bfloat16)


def fill_pattern(pattern_ref):
    shape = pattern_ref.shape
    pattern_ref[...] = (
        lax.broadcasted_iota(jnp.int32, shape, 0) * col_factor
        + lax.broadcasted_iota(jnp.int32, shape, 1) * row_factor
    )


def hash_rows(pattern_ref, out_ref, base, row, width):
    offset = base + (wrapped(row * col_factor) if isinstance(row, int) else row * col_factor)
    for first in range(0, width, sub_cols):
        last = min(first + sub_cols, width)
        out_ref[pl.ds(row, sub_rows), first:last] = to_gauss(pattern_ref[:, first:last] + offset)


def hash_tile(pattern_ref, out_ref, base, width):
    for row in range(0, tile, sub_rows):
        hash_rows(pattern_ref, out_ref, base, row, width)


def dot_nt(lhs, rhs):
    return lax.dot_general(
        lhs, rhs, (((1,), (1,)), ((), ())), preferred_element_type=jnp.float32
    )


def hash_kernel(bases_ref, out_ref, pattern_ref):
    step = pl.program_id(0)

    @pl.when(step == 0)
    def _():
        fill_pattern(pattern_ref)

    base = bases_ref[0] + step * wrapped(tile * col_factor)

    def strip(number, carry):
        row = pl.multiple_of(number * sub_rows, sub_rows)
        hash_rows(pattern_ref, out_ref, base, row, out_ref.shape[1])
        return carry

    lax.fori_loop(0, tile // sub_rows, strip, 0, unroll=4)


def hash_block(base, width, dims):
    return pl.pallas_call(
        hash_kernel,
        grid=(dims // tile,),
        in_specs=[pl.BlockSpec(memory_space=pltpu.SMEM)],
        out_specs=pl.BlockSpec((tile, width), lambda step: (step, 0)),
        out_shape=jax.ShapeDtypeStruct((dims, width), jnp.bfloat16),
        scratch_shapes=[pltpu.VMEM((sub_rows, width), jnp.int32)],
        cost_estimate=pl.CostEstimate(
            flops=18 * dims * width, bytes_accessed=2 * dims * width, transcendentals=0
        ),
        name="hash_block",
    )(base[None])


def early_kernel(blocks, bases_ref, *refs):
    acts = refs[:blocks]
    backs_ref = refs[blocks]
    u_refs = refs[blocks + 1 : 2 * blocks + 1]
    total_ref, gram_a_ref, gram_b_ref = refs[2 * blocks + 1 : 2 * blocks + 4]
    pattern_ref = refs[2 * blocks + 4]
    row_tiles = refs[2 * blocks + 5 : 3 * blocks + 5]
    col_tiles = refs[3 * blocks + 5 :]
    step = pl.program_id(0)
    rows = acts[0].shape[1]
    width = backs_ref.shape[1]
    tokens = gram_a_ref.shape[1]

    def row_base(block, at):
        return bases_ref[2 * block] + at * wrapped(tile * col_factor)

    @pl.when(step == 0)
    def _():
        fill_pattern(pattern_ref)
        hash_tile(pattern_ref, row_tiles[0], row_base(0, 0), rows)
        for e in range(gram_a_ref.shape[0]):
            here = slice(e * tokens, (e + 1) * tokens)
            gram = dot_nt(acts[0][here, :], acts[0][here, :])
            for block in range(1, blocks):
                gram += dot_nt(acts[block][here, :], acts[block][here, :])
            gram_a_ref[e] = gram
            gram_b_ref[e] = dot_nt(backs_ref[here, :], backs_ref[here, :])

    total = None
    for block in range(blocks):
        hash_tile(
            pattern_ref,
            col_tiles[block],
            bases_ref[2 * block + 1] + step * wrapped(tile * col_factor),
            width,
        )
        left = dot_nt(row_tiles[block][...], acts[block][...])
        u_refs[block][...] = left
        following = block + 1
        if following < blocks:
            hash_tile(pattern_ref, row_tiles[following], row_base(following, step), rows)
        else:
            hash_tile(pattern_ref, row_tiles[0], row_base(0, step + 1), rows)
        product = left * dot_nt(col_tiles[block][...], backs_ref[...])
        total = product if total is None else total + product
    total_ref[...] = total


def early(bases, acts, backs, examples, dims):
    blocks = len(acts)
    lanes, rows = acts[0].shape
    width = backs.shape[1]
    tokens = lanes // examples
    whole = lambda array: pl.BlockSpec(array.shape, lambda step: (0, 0))
    by_dims = pl.BlockSpec((tile, lanes), lambda step: (step, 0))
    gram_spec = pl.BlockSpec((examples, tokens, tokens), lambda step: (0, 0, 0))
    gram_shape = jax.ShapeDtypeStruct((examples, tokens, tokens), jnp.float32)
    dims_shape = jax.ShapeDtypeStruct((dims, lanes), jnp.float32)
    hashes = blocks * dims * (rows + width)
    return pl.pallas_call(
        functools.partial(early_kernel, blocks),
        grid=(dims // tile,),
        in_specs=[pl.BlockSpec(memory_space=pltpu.SMEM)]
        + [whole(block) for block in acts]
        + [whole(backs)],
        out_specs=[by_dims] * (blocks + 1) + [gram_spec] * 2,
        out_shape=[dims_shape] * (blocks + 1) + [gram_shape] * 2,
        scratch_shapes=[pltpu.VMEM((sub_rows, max(rows, width)), jnp.int32)]
        + [pltpu.VMEM((tile, rows), jnp.bfloat16)] * blocks
        + [pltpu.VMEM((tile, width), jnp.bfloat16)] * blocks,
        compiler_params=pltpu.CompilerParams(vmem_limit_bytes=40 * 2**20),
        cost_estimate=pl.CostEstimate(
            flops=18 * hashes + 2 * hashes * lanes,
            bytes_accessed=4 * dims * lanes * (blocks + 1),
            transcendentals=0,
        ),
        name="early",
    )(bases, *acts, backs)


def late_kernel(blocks, parts, has_late, place_ref, *refs):
    u_refs = refs[:blocks]
    total_ref, gram_a_ref, gram_b_ref = refs[blocks : blocks + 3]
    refs = refs[blocks + 3 :]
    if has_late:
        backs_ref, col_refs = refs[0], refs[1 : 1 + blocks]
        refs = refs[1 + blocks :]
    outs = refs[:parts]
    step = pl.program_id(0)
    examples, tokens = gram_a_ref.shape[:2]
    part_dims = outs[0].shape[2] - 128

    @pl.when(step == 0)
    def _():
        for e in range(examples):
            gram_b = gram_b_ref[e]
            if has_late:
                here = backs_ref[e * tokens : (e + 1) * tokens, :]
                gram_b = gram_b + dot_nt(here, here)
            both = jnp.sum(gram_a_ref[e] * gram_b)
            for out in outs:
                out[e, :, part_dims:] = jnp.full((1, 128), both, jnp.float32)

    total = total_ref[...]
    if has_late:
        for block in range(blocks):
            total += u_refs[block][...] * dot_nt(col_refs[block][...], backs_ref[...])
    step_dims = min(tile, part_dims)
    for e in range(examples):
        lane_sum = total[:, e * tokens : e * tokens + 128]
        for first in range(128, tokens, 128):
            lane_sum += total[:, e * tokens + first : e * tokens + first + 128]
        across = jnp.sum(lane_sum.T, axis=0, keepdims=True)
        for piece in range(0, tile, step_dims):
            number = (step * tile + piece) // part_dims
            inside = lax.rem(step * tile + piece, part_dims)
            slot = lax.rem(number - place_ref[0] + parts, parts)
            for which, out in enumerate(outs):

                @pl.when(slot == which)
                def _():
                    for begin in range(0, part_dims, step_dims):

                        @pl.when(inside == begin)
                        def _():
                            out[e, :, begin : begin + step_dims] = across[
                                :, piece : piece + step_dims
                            ]


def late(place, us, total, grams, backs, cols, examples, parts):
    blocks = len(us)
    dims, lanes = total.shape
    tokens = lanes // examples
    by_dims = pl.BlockSpec((tile, lanes), lambda step: (step, 0))
    gram_spec = pl.BlockSpec((examples, tokens, tokens), lambda step: (0, 0, 0))
    has_late = backs is not None
    operands = [place, *us, total, *grams]
    specs = [pl.BlockSpec(memory_space=pltpu.SMEM)] + [by_dims] * (blocks + 1) + [gram_spec] * 2
    if has_late:
        width = backs.shape[1]
        operands += [backs, *cols]
        specs += [pl.BlockSpec(backs.shape, lambda step: (0, 0))]
        specs += [pl.BlockSpec((tile, width), lambda step: (step, 0))] * blocks
    message = (examples, 1, dims // parts + 128)
    return pl.pallas_call(
        functools.partial(late_kernel, blocks, parts, has_late),
        grid=(dims // tile,),
        in_specs=specs,
        out_specs=[pl.BlockSpec(message, lambda step: (0, 0, 0))] * parts,
        out_shape=[jax.ShapeDtypeStruct(message, jnp.float32)] * parts,
        compiler_params=pltpu.CompilerParams(vmem_limit_bytes=40 * 2**20),
        name="late",
    )(*operands)


def on_device(parts, activations, backprops, block_counters):
    row_block = activations.shape[2]
    col_block = backprops.shape[2]
    place = lax.axis_index("param")
    acts = activations[0]
    backs = backprops[0]
    counters = block_counters[:, 0]

    def bases_of(streams, place_of, early_at):
        row_start = streams[0] * stream_factor + place_of * wrapped(row_block * row_factor)
        col_start = streams[1] * stream_factor
        return row_start, col_start + early_at * wrapped(col_block * row_factor)

    if parts == 4:
        swap = [(0, 1), (1, 0), (2, 3), (3, 2)]
        other_counters = lax.ppermute(block_counters, "param", swap)[:, 0]
        other_acts = lax.ppermute(acts, "param", swap)
        early_backs = lax.ppermute(backs, "param", [(0, 0), (1, 2), (2, 1), (3, 3)])
        other = jnp.bitwise_xor(place, 1)
        early_at = jnp.array([0, 2, 1, 3], jnp.int32)[place]
        late_at = jnp.array([1, 3, 0, 2], jnp.int32)[place]
        late_step = wrapped(col_block * row_factor)
        own_col = counters[1] * stream_factor
        other_col = other_counters[1] * stream_factor
        own_late = hash_block(own_col + late_at * late_step, col_block, K)
        late_backs = lax.ppermute(backs, "param", [(0, 2), (3, 1), (1, 0), (2, 3)])
        other_late = hash_block(other_col + late_at * late_step, col_block, K)
        bases = jnp.stack(
            [*bases_of(counters, place, early_at), *bases_of(other_counters, other, early_at)]
        )
        results = early(bases, [acts, other_acts], early_backs, 1, K)
        late_cols = [own_late, other_late]
    else:
        every_back = lax.all_gather(backs, "param", axis=1, tiled=True)
        bases = jnp.stack(bases_of(counters, place, 0))
        results = early(bases, [acts], every_back, 1, K)
        late_backs, late_cols = None, None
    *us, total, gram_a, gram_b = results
    messages = late(place[None], us, total, (gram_a, gram_b), late_backs, late_cols, 1, parts)
    summed = messages[0]
    for distance in range(1, parts):
        moves = [(source, (source + distance) % parts) for source in range(parts)]
        summed = summed + lax.ppermute(messages[distance], "param", moves)
    part_dims = K // parts
    sumsq = jnp.maximum(summed[:, 0, part_dims], 0.0)
    features = summed[:, 0, :part_dims] * (lax.rsqrt(sumsq + epsilon) * unscale)[:, None]
    return (features, jnp.sqrt(sumsq))


def solution(mesh):
    return jax.shard_map(
        functools.partial(on_device, mesh.shape["param"]),
        mesh=mesh,
        in_specs=(
            P(("grp", "ex"), None, "param"),
            P(("grp", "ex"), None, "param"),
            P(None, "param"),
        ),
        out_specs=(P(("grp", "ex"), "param"), P(("grp", "ex"))),
        check_vma=False,
    )
```

```python
import functools

import jax
import jax.numpy as jnp
from jax import lax
from jax.experimental import pallas as pl
from jax.experimental.pallas import tpu as pltpu
from jax.sharding import PartitionSpec as P

K = 2048

mix_factor = 73244475
stream_factor = 668265261
row_factor = 374761393
col_factor = 1103515245
epsilon = 1e-06
unscale = 1.0 / (128.0 * 128.0)

tile = 256
sub_rows = 16
sub_cols = 256


def wrapped(number):
    return jnp.int32((number + 2**31) % 2**32 - 2**31)


def scramble(hashed):
    sixteen = jnp.int32(16)
    hashed = jnp.bitwise_xor(hashed, lax.shift_right_logical(hashed, sixteen))
    hashed = hashed * mix_factor
    hashed = jnp.bitwise_xor(hashed, lax.shift_right_logical(hashed, sixteen))
    hashed = hashed * mix_factor
    return jnp.bitwise_xor(hashed, lax.shift_right_logical(hashed, sixteen))


def to_gauss(hashed):
    hashed = scramble(hashed)
    pairs = jnp.int32(0x00FF00FF)
    two_sums = jnp.bitwise_and(hashed, pairs) + jnp.bitwise_and(
        lax.shift_right_logical(hashed, jnp.int32(8)), pairs
    )
    total = lax.shift_right_logical(two_sums * jnp.int32(0x10001), jnp.int32(16))
    return (total - 510).astype(jnp.float32).astype(jnp.bfloat16)


def fill_pattern(pattern_ref):
    shape = pattern_ref.shape
    pattern_ref[...] = (
        lax.broadcasted_iota(jnp.int32, shape, 0) * col_factor
        + lax.broadcasted_iota(jnp.int32, shape, 1) * row_factor
    )


def hash_rows(pattern_ref, out_ref, base, row, width):
    offset = base + (wrapped(row * col_factor) if isinstance(row, int) else row * col_factor)
    for first in range(0, width, sub_cols):
        last = min(first + sub_cols, width)
        out_ref[pl.ds(row, sub_rows), first:last] = to_gauss(pattern_ref[:, first:last] + offset)


def hash_tile(pattern_ref, out_ref, base):
    rows, width = out_ref.shape
    for row in range(0, rows, sub_rows):
        hash_rows(pattern_ref, out_ref, base, row, width)


def dot_nt(lhs, rhs):
    return lax.dot_general(
        lhs, rhs, (((1,), (1,)), ((), ())), preferred_element_type=jnp.float32
    )


def row_base(counters_ref, place, rows):
    return counters_ref[0, 0] * stream_factor + place * wrapped(rows * row_factor)


def col_base(counters_ref, place, columns):
    return counters_ref[1, 0] * stream_factor + place * wrapped(columns * row_factor)


def first_dim(halves, dims):
    if halves == 1:
        return jnp.int32(0)
    return lax.rem(lax.axis_index("ex"), halves) * wrapped(dims * col_factor)


def places(parts):
    place = lax.axis_index("param")
    if parts != 4:
        return place, place, jnp.int32(0), jnp.int32(0)
    early_at = 2 * jnp.bitwise_and(place, 1) + lax.shift_right_logical(place, 1)
    return place, jnp.bitwise_xor(place, 1), early_at, jnp.bitwise_xor(early_at, 1)


def rows_at(step, size):
    return pl.ds(pl.multiple_of(step * size, size), size)


def stream(steps, hashes, uses, beside_first=None):
    hashes[0](0)
    if beside_first is not None:
        beside_first()

    def run(step, last):
        for number, use in enumerate(uses):
            if number + 1 < len(uses):
                hashes[number + 1](step)
            elif not last:
                hashes[0](step + 1)
            use(step)

    def body(step, carry):
        run(step, False)
        return carry

    lax.fori_loop(0, steps - 1, body, 0)
    run(steps - 1, True)


def call(kernel, name, in_smem, operands, outs, scratch, flops, megabytes):
    specs = [pl.BlockSpec(memory_space=pltpu.SMEM)] * in_smem
    specs += [pl.BlockSpec(memory_space=pltpu.VMEM)] * (len(operands) - in_smem)
    return pl.pallas_call(
        kernel,
        in_specs=specs,
        out_specs=[pl.BlockSpec(memory_space=pltpu.VMEM)] * len(outs),
        out_shape=outs,
        scratch_shapes=scratch,
        compiler_params=pltpu.CompilerParams(vmem_limit_bytes=megabytes * 2**20),
        cost_estimate=pl.CostEstimate(flops=flops, bytes_accessed=0, transcendentals=0),
        name=name,
    )(*operands)


def ahead_kernel(parts, halves, is_row, counters_ref, out_ref, pattern_ref):
    _, partner, _, late_at = places(parts)
    dims, columns = out_ref.shape
    fill_pattern(pattern_ref)
    if is_row:
        base = row_base(counters_ref, partner, columns)
    else:
        base = col_base(counters_ref, late_at, columns)
    base += first_dim(halves, dims)

    def strip(number, carry):
        row = pl.multiple_of(number * sub_rows, sub_rows)
        hash_rows(pattern_ref, out_ref, base, row, columns)
        return carry

    lax.fori_loop(0, dims // sub_rows, strip, 0, unroll=4)


def ahead(parts, halves, is_row, counters, columns, dims):
    (block,) = call(
        functools.partial(ahead_kernel, parts, halves, is_row),
        "ahead",
        1,
        [counters],
        [jax.ShapeDtypeStruct((dims, columns), jnp.bfloat16)],
        [pltpu.VMEM((sub_rows, columns), jnp.int32)],
        1000 * dims * columns,
        8,
    )
    return block


def left_kernel(parts, halves, examples, own_ref, *refs):
    acts = refs[:examples]
    u_ref, pattern_ref = refs[examples : examples + 2]
    tiles = refs[examples + 2 :]
    tokens, rows = acts[0].shape
    dims = u_ref.shape[0]
    piece = tiles[0].shape[0]
    fill_pattern(pattern_ref)
    base = row_base(own_ref, places(parts)[0], rows) + first_dim(halves, dims)

    def hash_into(number):
        def run(step):
            offset = step * wrapped(tile * col_factor) + wrapped(number * piece * col_factor)
            hash_tile(pattern_ref, tiles[number], base + offset)

        return run

    def use(number):
        def run(step):
            for e in range(examples):
                u_ref[rows_at(step * len(tiles) + number, piece), e * tokens : (e + 1) * tokens] = (
                    dot_nt(tiles[number][...], acts[e][...])
                )

        return run

    numbers = range(len(tiles))
    stream(dims // tile, [hash_into(n) for n in numbers], [use(n) for n in numbers])


def left(parts, halves, own, acts, dims):
    examples = len(acts)
    tokens, rows = acts[0].shape
    lanes = examples * tokens
    pieces = 2
    (u_own,) = call(
        functools.partial(left_kernel, parts, halves, examples),
        "left",
        1,
        [own, *acts],
        [jax.ShapeDtypeStruct((dims, lanes), jnp.float32)],
        [pltpu.VMEM((sub_rows, rows), jnp.int32)]
        + [pltpu.VMEM((tile // pieces, rows), jnp.bfloat16)] * pieces,
        1000 * dims * rows,
        16,
    )
    return u_own


def middle_kernel(parts, halves, examples, blocks, *refs):
    counters, refs = refs[:blocks], refs[blocks:]
    acts = [refs[b * examples : (b + 1) * examples] for b in range(blocks)]
    refs = refs[blocks * examples :]
    backs, refs = refs[:examples], refs[examples:]
    u_own, refs = refs[0], refs[1:]
    if blocks == 2:
        row_other, u_other, refs = refs[0], refs[1], refs[2:]
    total_ref, gram_a_ref, gram_b_ref, pattern_ref = refs[:4]
    tiles = refs[4:]
    dims = u_own.shape[0]
    tokens, columns = backs[0].shape
    _, _, early_at, _ = places(parts)
    fill_pattern(pattern_ref)

    def grams():
        for e in range(examples):
            gram = None
            for block in acts:
                term = dot_nt(block[e][...], block[e][...])
                gram = term if gram is None else gram + term
            gram_a_ref[e] = gram
            gram_b_ref[e] = dot_nt(backs[e][...], backs[e][...])

    def hash_into(block):
        base = col_base(counters[block], early_at, columns) + first_dim(halves, dims)

        def run(step):
            hash_tile(pattern_ref, tiles[block], base + step * wrapped(tile * col_factor))

        return run

    def use_own(step):
        rows = rows_at(step, tile)
        for e in range(examples):
            here = slice(e * tokens, (e + 1) * tokens)
            total_ref[rows, here] = u_own[rows, here] * dot_nt(tiles[0][...], backs[e][...])

    def use_other(step):
        rows = rows_at(step, tile)
        for e in range(examples):
            here = slice(e * tokens, (e + 1) * tokens)
            u_piece = dot_nt(row_other[rows, :], acts[1][e][...])
            u_other[rows, here] = u_piece
            total_ref[rows, here] += u_piece * dot_nt(tiles[1][...], backs[e][...])

    stream(
        dims // tile, [hash_into(b) for b in range(blocks)], [use_own, use_other][:blocks], grams
    )


def middle(parts, halves, counters, acts, backs, u_own, row_other):
    blocks = len(counters)
    examples = len(backs)
    tokens, columns = backs[0].shape
    dims, lanes = u_own.shape
    gram_shape = jax.ShapeDtypeStruct((examples, tokens, tokens), jnp.float32)
    dims_shape = jax.ShapeDtypeStruct((dims, lanes), jnp.float32)
    operands = [*counters, *[a for block in acts for a in block], *backs, u_own]
    if blocks == 2:
        operands.append(row_other)
    return call(
        functools.partial(middle_kernel, parts, halves, examples, blocks),
        "middle",
        blocks,
        operands,
        [dims_shape] * blocks + [gram_shape] * 2,
        [pltpu.VMEM((sub_rows, columns), jnp.int32)]
        + [pltpu.VMEM((tile, columns), jnp.bfloat16)] * blocks,
        1000 * blocks * dims * columns,
        24,
    )


def late_kernel(parts, halves, examples, blocks, *refs):
    u_refs, refs = refs[:blocks], refs[blocks:]
    total_ref, gram_a_ref, gram_b_ref = refs[:3]
    refs = refs[3:]
    backs = ()
    if blocks:
        backs, refs = refs[:examples], refs[examples:]
        cols, refs = refs[:blocks], refs[blocks:]
    outs = refs
    tokens = gram_a_ref.shape[1]
    dims = total_ref.shape[0]
    part_dims = outs[0].shape[1] - 128
    place = lax.axis_index("param")
    if halves == 2:
        core = lax.rem(lax.axis_index("ex"), 2)

    def send(e, number, columns, values):
        if halves == 1:
            slot = lax.rem(number - place + parts, parts)
        else:
            slot = jnp.bitwise_xor(2 * number + jnp.bitwise_xor(core, e), place)
        for which, out in enumerate(outs):

            @pl.when(slot == which)
            def _():
                out[:, columns] = values

    across = []
    for e in range(examples):
        here = slice(e * tokens, (e + 1) * tokens)
        for step in range(dims // tile):
            rows = slice(step * tile, (step + 1) * tile)
            total = total_ref[rows, here]
            for block in range(blocks):
                total += u_refs[block][rows, here] * dot_nt(cols[block][rows, :], backs[e][...])
            lane_sum = total[:, :128]
            for begin in range(128, tokens, 128):
                lane_sum += total[:, begin : begin + 128]
            across.append(jnp.sum(lane_sum.T, axis=0, keepdims=True))
    for e in range(examples):
        gram_b = gram_b_ref[e]
        if blocks:
            gram_b = gram_b + dot_nt(backs[e][...], backs[e][...])
        both = jnp.full((1, 128), jnp.sum(gram_a_ref[e] * gram_b), jnp.float32)
        for number in range(parts // halves):
            send(e, number, slice(part_dims, part_dims + 128), both)
            step_dims = min(tile, part_dims)
            for begin in range(0, part_dims, step_dims):
                at = number * part_dims + begin
                step, inside = divmod(at, tile)
                values = across[e * (dims // tile) + step][:, inside : inside + step_dims]
                send(e, number, slice(begin, begin + step_dims), values)


def late(parts, halves, us, total, grams, backs, cols):
    blocks = len(cols)
    dims, lanes = total.shape
    examples, tokens = grams[0].shape[:2]
    message = jax.ShapeDtypeStruct((1, dims * halves // parts + 128), jnp.float32)
    return call(
        functools.partial(late_kernel, parts, halves, examples, blocks),
        "late",
        0,
        [*us[:blocks], total, *grams, *backs, *cols],
        [message] * parts,
        [],
        2 * blocks * dims * lanes * 1024,
        24,
    )


def on_device(parts, group, activations, backprops, block_counters):
    columns = backprops.shape[2]
    acts = activations[0]
    backs = backprops[0]
    if parts == 4 and group % 2 == 0:
        swap = [(0, 1), (1, 0), (2, 3), (3, 2)]
        halves = 2
        dims = K // halves

        def with_sibling(array):
            pairs = [(device, device ^ 1) for device in range(group)]
            return [array, lax.ppermute(array, "ex", pairs)]

        other_counters = lax.ppermute(block_counters, "param", swap)
        early_backs = lax.ppermute(backs, "param", [(0, 0), (1, 2), (2, 1), (3, 3)])
        own_pair = with_sibling(acts)
        late_own = ahead(parts, halves, False, block_counters, columns, dims)
        acts, backs, late_own, other_counters = lax.optimization_barrier(
            (acts, backs, late_own, other_counters)
        )
        other_acts = lax.ppermute(acts, "param", swap)
        late_backs = lax.ppermute(backs, "param", [(0, 2), (3, 1), (1, 0), (2, 3)])
        u_own = left(parts, halves, block_counters, own_pair, dims)
        late_other = ahead(parts, halves, False, other_counters, columns, dims)
        other_acts, early_backs, u_own, late_other = lax.optimization_barrier(
            (other_acts, early_backs, u_own, late_other)
        )
        other_pair = with_sibling(other_acts)
        early_pair = with_sibling(early_backs)
        row_other = ahead(parts, halves, True, other_counters, columns, dims)
        u_other, total, *grams = middle(
            parts,
            halves,
            [block_counters, other_counters],
            [own_pair, other_pair],
            early_pair,
            u_own,
            row_other,
        )
        late_pair = with_sibling(late_backs)
        messages = late(
            parts, halves, [u_own, u_other], total, grams, late_pair, [late_own, late_other]
        )
    else:
        halves = 1
        every_back = lax.all_gather(backs, "param", axis=1, tiled=True)
        u_own = left(parts, halves, block_counters, [acts], K)
        total, *grams = middle(
            parts, halves, [block_counters], [[acts]], [every_back], u_own, None
        )
        messages = late(parts, halves, [], total, grams, [], [])
    summed = None
    for number, message in enumerate(messages):
        if halves == 1:
            moves = [(source, (source + number) % parts) for source in range(parts)]
            moved = lax.ppermute(message, "param", moves) if number else message
        else:
            moves = [
                (
                    z * group + chip * 2 + core,
                    (2 * core + (z ^ number) // 2) * group + chip * 2 + (z ^ number) % 2,
                )
                for z in range(parts)
                for chip in range(group // 2)
                for core in range(2)
            ]
            moved = lax.ppermute(message, ("param", "ex"), moves)
        summed = moved if summed is None else summed + moved
    part_dims = K // parts
    sumsq = jnp.maximum(summed[:, part_dims], 0.0)
    features = summed[:, :part_dims] * (lax.rsqrt(sumsq + epsilon) * unscale)[:, None]
    return (features, jnp.sqrt(sumsq))


def solution(mesh):
    return jax.shard_map(
        functools.partial(on_device, mesh.shape["param"], mesh.shape["ex"]),
        mesh=mesh,
        in_specs=(
            P(("grp", "ex"), None, "param"),
            P(("grp", "ex"), None, "param"),
            P(None, "param"),
        ),
        out_specs=(P(("grp", "ex"), "param"), P(("grp", "ex"))),
        check_vma=False,
    )
```

```python
import functools

import jax
import jax.numpy as jnp
from jax import lax
from jax.experimental import pallas as pl
from jax.experimental.pallas import tpu as pltpu
from jax.sharding import PartitionSpec as P

K = 2048

mix_factor = 73244475
stream_factor = 668265261
row_factor = 374761393
col_factor = 1103515245
epsilon = 1e-06
unscale = 1.0 / (128.0 * 128.0)

tile = 256
sub_rows = 16
sub_cols = 256


def wrapped(number):
    return jnp.int32((number + 2**31) % 2**32 - 2**31)


def scramble(hashed):
    sixteen = jnp.int32(16)
    hashed = jnp.bitwise_xor(hashed, lax.shift_right_logical(hashed, sixteen))
    hashed = hashed * mix_factor
    hashed = jnp.bitwise_xor(hashed, lax.shift_right_logical(hashed, sixteen))
    hashed = hashed * mix_factor
    return jnp.bitwise_xor(hashed, lax.shift_right_logical(hashed, sixteen))


def to_gauss(hashed):
    hashed = scramble(hashed)
    pairs = jnp.int32(0x00FF00FF)
    two_sums = jnp.bitwise_and(hashed, pairs) + jnp.bitwise_and(
        lax.shift_right_logical(hashed, jnp.int32(8)), pairs
    )
    total = lax.shift_right_logical(two_sums * jnp.int32(0x10001), jnp.int32(16))
    return (total - 510).astype(jnp.float32).astype(jnp.bfloat16)


def fill_pattern(pattern_ref):
    shape = pattern_ref.shape
    pattern_ref[...] = (
        lax.broadcasted_iota(jnp.int32, shape, 0) * col_factor
        + lax.broadcasted_iota(jnp.int32, shape, 1) * row_factor
    )


def hash_rows(pattern_ref, out_ref, base, row, width):
    offset = base + (wrapped(row * col_factor) if isinstance(row, int) else row * col_factor)
    for first in range(0, width, sub_cols):
        last = min(first + sub_cols, width)
        out_ref[pl.ds(row, sub_rows), first:last] = to_gauss(pattern_ref[:, first:last] + offset)


def hash_tile(pattern_ref, out_ref, base):
    rows, width = out_ref.shape
    for row in range(0, rows, sub_rows):
        hash_rows(pattern_ref, out_ref, base, row, width)


def dot_nt(lhs, rhs):
    return lax.dot_general(
        lhs, rhs, (((1,), (1,)), ((), ())), preferred_element_type=jnp.float32
    )


def counter(source, which):
    if source.dtype == jnp.int32:
        return source[which, 0]
    row = source[source.shape[0] - 16 :, 0:128].astype(jnp.float32)[0:1]
    lane = lax.broadcasted_iota(jnp.int32, row.shape, 1) - 3 * which
    zero = jnp.zeros_like(row)
    value = zero
    for digit in range(3):
        value += jnp.where(lane == digit, row * float(256**digit), zero)
    return jnp.sum(value).astype(jnp.int32)


def row_base(source, place, rows):
    return counter(source, 0) * stream_factor + place * wrapped(rows * row_factor)


def col_base(source, place, columns):
    return counter(source, 1) * stream_factor + place * wrapped(columns * row_factor)


def first_dim(halves, dims):
    if halves == 1:
        return jnp.int32(0)
    return lax.rem(lax.axis_index("ex"), halves) * wrapped(dims * col_factor)


def places(parts):
    place = lax.axis_index("param")
    if parts != 4:
        return place, place, jnp.int32(0), jnp.int32(0)
    early_at = 2 * jnp.bitwise_and(place, 1) + lax.shift_right_logical(place, 1)
    return place, jnp.bitwise_xor(place, 1), early_at, jnp.bitwise_xor(early_at, 1)


def rows_at(step, size):
    return pl.ds(pl.multiple_of(step * size, size), size)


def stream(steps, hash_at, use, beside_first):
    hash_at(0, 0)
    beside_first()

    def body(turn, carry):
        hash_at(2 * turn + 1, 1)
        use(2 * turn, 0)
        hash_at(2 * turn + 2, 0)
        use(2 * turn + 1, 1)
        return carry

    lax.fori_loop(0, steps // 2 - 1, body, 0)
    hash_at(steps - 1, 1)
    use(steps - 2, 0)
    use(steps - 1, 1)


def call(kernel, name, operands, outs, scratch, flops, megabytes):
    spaces = [pltpu.SMEM if array.dtype == jnp.int32 else pltpu.VMEM for array in operands]
    return pl.pallas_call(
        kernel,
        in_specs=[pl.BlockSpec(memory_space=space) for space in spaces],
        out_specs=[pl.BlockSpec(memory_space=pltpu.VMEM)] * len(outs),
        out_shape=outs,
        scratch_shapes=scratch,
        compiler_params=pltpu.CompilerParams(vmem_limit_bytes=megabytes * 2**20),
        cost_estimate=pl.CostEstimate(flops=flops, bytes_accessed=0, transcendentals=0),
        name=name,
    )(*operands)


def floats(*shape):
    return jax.ShapeDtypeStruct(shape, jnp.float32)


def digits_kernel(acts_ref, counters_ref, out_ref):
    tokens, rows = acts_ref.shape
    out_ref[:tokens, :] = acts_ref[...]
    lane = lax.broadcasted_iota(jnp.int32, (16, rows), 1)
    digits = jnp.zeros((16, rows), jnp.int32)
    for which in range(2):
        for digit in range(3):
            value = lax.shift_right_logical(counters_ref[which, 0], jnp.int32(8 * digit))
            digits = jnp.where(lane == 3 * which + digit, jnp.bitwise_and(value, 255), digits)
    out_ref[tokens:, :] = digits.astype(jnp.float32).astype(out_ref.dtype)


def with_digits(acts, counters):
    tokens, rows = acts.shape
    (out,) = call(
        digits_kernel,
        "with_digits",
        [acts, counters],
        [jax.ShapeDtypeStruct((tokens + 16, rows), acts.dtype)],
        [],
        0,
        8,
    )
    return out


def ahead_kernel(parts, halves, is_row, source, out_ref, pattern_ref):
    _, partner, _, late_at = places(parts)
    dims, columns = out_ref.shape
    fill_pattern(pattern_ref)
    if is_row:
        base = row_base(source, partner, columns)
    else:
        base = col_base(source, late_at, columns)
    base += first_dim(halves, dims)

    def strip(number, carry):
        row = pl.multiple_of(number * sub_rows, sub_rows)
        hash_rows(pattern_ref, out_ref, base, row, columns)
        return carry

    lax.fori_loop(0, dims // sub_rows, strip, 0, unroll=4)


def ahead(parts, halves, is_row, source, columns, dims):
    (block,) = call(
        functools.partial(ahead_kernel, parts, halves, is_row),
        "ahead",
        [source],
        [jax.ShapeDtypeStruct((dims, columns), jnp.bfloat16)],
        [pltpu.VMEM((sub_rows, columns), jnp.int32)],
        1000 * dims * columns,
        8,
    )
    return block


def left_kernel(parts, halves, examples, source, *refs):
    acts = refs[:examples]
    u_ref, gram_ref, pattern_ref = refs[examples : examples + 3]
    tiles = refs[examples + 3 :]
    tokens, rows = acts[0].shape
    dims = u_ref.shape[0]
    fill_pattern(pattern_ref)
    base = row_base(source, places(parts)[0], rows) + first_dim(halves, dims)

    def hash_at(step, which):
        hash_tile(pattern_ref, tiles[which], base + step * wrapped(tile * col_factor))

    def grams():
        for e in range(examples):
            gram_ref[e] = dot_nt(acts[e][...], acts[e][...])

    def use(step, which):
        for e in range(examples):
            u_ref[rows_at(step, tile), e * tokens : (e + 1) * tokens] = dot_nt(
                tiles[which][...], acts[e][...]
            )

    stream(dims // tile, hash_at, use, grams)


def left(parts, halves, own, acts, dims):
    examples = len(acts)
    tokens, rows = acts[0].shape
    return call(
        functools.partial(left_kernel, parts, halves, examples),
        "left",
        [own, *acts],
        [floats(dims, examples * tokens), floats(examples, tokens, tokens)],
        [pltpu.VMEM((sub_rows, rows), jnp.int32)] + [pltpu.VMEM((tile, rows), jnp.bfloat16)] * 2,
        1000 * dims * rows,
        16,
    )


def middle_kernel(parts, halves, examples, paired, source, *refs):
    if paired:
        acts, refs = (source, *refs[: examples - 1]), refs[examples - 1 :]
        row_ref, total_in, refs = refs[0], refs[1], refs[2:]
    else:
        u_ref, refs = refs[0], refs[1:]
    backs, refs = refs[:examples], refs[examples:]
    total_ref, gram_ref, refs = refs[0], refs[1], refs[2:]
    if paired:
        u_ref, refs = refs[0], refs[1:]
    pattern_ref, tiles = refs[0], refs[1:]
    dims = total_ref.shape[0]
    tokens, columns = backs[0].shape
    _, _, early_at, _ = places(parts)
    fill_pattern(pattern_ref)
    base = col_base(source, early_at, columns) + first_dim(halves, dims)

    def hash_at(step, which):
        hash_tile(pattern_ref, tiles[which], base + step * wrapped(tile * col_factor))

    def grams():
        for e in range(examples):
            tokens_of = acts[e][:tokens, :] if paired else backs[e][...]
            gram_ref[e] = dot_nt(tokens_of, tokens_of)

    def use(step, which):
        rows = rows_at(step, tile)
        for e in range(examples):
            here = slice(e * tokens, (e + 1) * tokens)
            right = dot_nt(tiles[which][...], backs[e][...])
            if paired:
                u_piece = dot_nt(row_ref[rows, :], acts[e][:tokens, :])
                u_ref[rows, here] = u_piece
                total_ref[rows, here] = total_in[rows, here] + u_piece * right
            else:
                total_ref[rows, here] = u_ref[rows, here] * right

    stream(dims // tile, hash_at, use, grams)


def middle(parts, halves, source, backs, u_own=None, other=None):
    examples = len(backs)
    tokens, columns = backs[0].shape
    if other is None:
        operands = [source, u_own, *backs]
        dims = u_own.shape[0]
        more = []
    else:
        siblings, row_other, total = other
        operands = [source, *siblings, row_other, total, *backs]
        dims = total.shape[0]
        more = [floats(dims, examples * tokens)]
    return call(
        functools.partial(middle_kernel, parts, halves, examples, other is not None),
        "middle",
        operands,
        [floats(dims, examples * tokens), floats(examples, tokens, tokens), *more],
        [pltpu.VMEM((sub_rows, columns), jnp.int32)]
        + [pltpu.VMEM((tile, columns), jnp.bfloat16)] * 2,
        1000 * dims * columns,
        20,
    )


def late_kernel(parts, halves, examples, blocks, *refs):
    u_refs, refs = refs[:blocks], refs[blocks:]
    total_ref, refs = refs[0], refs[1:]
    sides = max(blocks, 1)
    grams_a, grams_b, refs = refs[:sides], refs[sides], refs[sides + 1 :]
    backs = ()
    if blocks:
        backs, refs = refs[:examples], refs[examples:]
        cols, refs = refs[:blocks], refs[blocks:]
    outs = refs
    tokens = grams_b.shape[1]
    dims = total_ref.shape[0]
    part_dims = outs[0].shape[1] - 128
    place = lax.axis_index("param")
    if halves == 2:
        core = lax.rem(lax.axis_index("ex"), 2)

    def send(e, number, columns, values):
        if halves == 1:
            slot = lax.rem(number - place + parts, parts)
        else:
            slot = jnp.bitwise_xor(2 * number + jnp.bitwise_xor(core, e), place)
        for which, out in enumerate(outs):

            @pl.when(slot == which)
            def _():
                out[:, columns] = values

    across = []
    for e in range(examples):
        here = slice(e * tokens, (e + 1) * tokens)
        for step in range(dims // tile):
            rows = slice(step * tile, (step + 1) * tile)
            total = total_ref[rows, here]
            for block in range(blocks):
                total += u_refs[block][rows, here] * dot_nt(cols[block][rows, :], backs[e][...])
            lane_sum = total[:, :128]
            for begin in range(128, tokens, 128):
                lane_sum += total[:, begin : begin + 128]
            across.append(jnp.sum(lane_sum.T, axis=0, keepdims=True))
    for e in range(examples):
        gram_a = grams_a[0][e]
        for more in grams_a[1:]:
            gram_a = gram_a + more[e]
        gram_b = grams_b[e]
        if blocks:
            gram_b = gram_b + dot_nt(backs[e][...], backs[e][...])
        both = jnp.full((1, 128), jnp.sum(gram_a * gram_b), jnp.float32)
        for number in range(parts // halves):
            send(e, number, slice(part_dims, part_dims + 128), both)
            step_dims = min(tile, part_dims)
            for begin in range(0, part_dims, step_dims):
                at = number * part_dims + begin
                step, inside = divmod(at, tile)
                values = across[e * (dims // tile) + step][:, inside : inside + step_dims]
                send(e, number, slice(begin, begin + step_dims), values)


def late(parts, halves, us, total, grams, backs, cols):
    blocks = len(cols)
    dims, lanes = total.shape
    examples, tokens = grams[0].shape[:2]
    message = jax.ShapeDtypeStruct((1, dims * halves // parts + 128), jnp.float32)
    return call(
        functools.partial(late_kernel, parts, halves, examples, blocks),
        "late",
        [*us[:blocks], total, *grams, *backs, *cols],
        [message] * parts,
        [],
        2 * blocks * dims * lanes * 1024,
        24,
    )


def on_device(parts, group, activations, backprops, block_counters):
    columns = backprops.shape[2]
    acts = activations[0]
    backs = backprops[0]
    if parts == 4 and group % 2 == 0:
        swap = [(0, 1), (1, 0), (2, 3), (3, 2)]
        halves = 2
        dims = K // halves

        def with_sibling(array):
            pairs = [(device, device ^ 1) for device in range(group)]
            return [array, lax.ppermute(array, "ex", pairs)]

        other_acts = lax.ppermute(with_digits(acts, block_counters), "param", swap)
        early_backs = lax.ppermute(backs, "param", [(0, 0), (1, 2), (2, 1), (3, 3)])
        own_pair = with_sibling(acts)
        late_own = ahead(parts, halves, False, block_counters, columns, dims)
        late_backs = lax.ppermute(backs, "param", [(0, 2), (3, 1), (1, 0), (2, 3)])
        u_own, gram_own = left(parts, halves, block_counters, own_pair, dims)
        other_acts, u_own, late_own = lax.optimization_barrier((other_acts, u_own, late_own))
        late_other = ahead(parts, halves, False, other_acts, columns, dims)
        row_other = ahead(parts, halves, True, other_acts, columns, dims)
        other_acts, early_backs, late_backs, late_other, row_other = lax.optimization_barrier(
            (other_acts, early_backs, late_backs, late_other, row_other)
        )
        early_pair = with_sibling(early_backs)
        other_pair = with_sibling(other_acts)
        late_pair = with_sibling(late_backs)
        total, gram_early = middle(parts, halves, block_counters, early_pair, u_own=u_own)
        total, gram_other, u_other = middle(
            parts, halves, other_acts, early_pair, other=(other_pair[1:], row_other, total)
        )
        messages = late(
            parts,
            halves,
            [u_own, u_other],
            total,
            [gram_own, gram_other, gram_early],
            late_pair,
            [late_own, late_other],
        )
    else:
        halves = 1
        every_back = lax.all_gather(backs, "param", axis=1, tiled=True)
        u_own, gram_own = left(parts, halves, block_counters, [acts], K)
        total, gram_backs = middle(parts, halves, block_counters, [every_back], u_own=u_own)
        messages = late(parts, halves, [], total, [gram_own, gram_backs], [], [])
    summed = None
    for number, message in enumerate(messages):
        if halves == 1:
            moves = [(source, (source + number) % parts) for source in range(parts)]
            moved = lax.ppermute(message, "param", moves) if number else message
        else:
            moves = [
                (
                    z * group + chip * 2 + core,
                    (2 * core + (z ^ number) // 2) * group + chip * 2 + (z ^ number) % 2,
                )
                for z in range(parts)
                for chip in range(group // 2)
                for core in range(2)
            ]
            moved = lax.ppermute(message, ("param", "ex"), moves)
        summed = moved if summed is None else summed + moved
    part_dims = K // parts
    sumsq = jnp.maximum(summed[:, part_dims], 0.0)
    features = summed[:, :part_dims] * (lax.rsqrt(sumsq + epsilon) * unscale)[:, None]
    return (features, jnp.sqrt(sumsq))


def solution(mesh):
    return jax.shard_map(
        functools.partial(on_device, mesh.shape["param"], mesh.shape["ex"]),
        mesh=mesh,
        in_specs=(
            P(("grp", "ex"), None, "param"),
            P(("grp", "ex"), None, "param"),
            P(None, "param"),
        ),
        out_specs=(P(("grp", "ex"), "param"), P(("grp", "ex"))),
        check_vma=False,
    )
```

```python
import functools

import jax
import jax.numpy as jnp
from jax import lax
from jax.experimental import pallas as pl
from jax.experimental.pallas import tpu as pltpu
from jax.sharding import PartitionSpec as P

K = 2048

mix_factor = 73244475
stream_factor = 668265261
row_factor = 374761393
col_factor = 1103515245
epsilon = 1e-06
unscale = 1.0 / (128.0 * 128.0)

tile = 256
sub_rows = 16
sub_cols = 256


def wrapped(number):
    return jnp.int32((number + 2**31) % 2**32 - 2**31)


def scramble(hashed):
    sixteen = jnp.int32(16)
    hashed = jnp.bitwise_xor(hashed, lax.shift_right_logical(hashed, sixteen))
    hashed = hashed * mix_factor
    hashed = jnp.bitwise_xor(hashed, lax.shift_right_logical(hashed, sixteen))
    hashed = hashed * mix_factor
    return jnp.bitwise_xor(hashed, lax.shift_right_logical(hashed, sixteen))


def to_gauss(hashed):
    hashed = scramble(hashed)
    pairs = jnp.int32(0x00FF00FF)
    two_sums = jnp.bitwise_and(hashed, pairs) + jnp.bitwise_and(
        lax.shift_right_logical(hashed, jnp.int32(8)), pairs
    )
    total = lax.shift_right_logical(two_sums * jnp.int32(0x10001), jnp.int32(16))
    return (total - 510).astype(jnp.float32).astype(jnp.bfloat16)


def fill_pattern(pattern_ref):
    shape = pattern_ref.shape
    pattern_ref[...] = (
        lax.broadcasted_iota(jnp.int32, shape, 0) * col_factor
        + lax.broadcasted_iota(jnp.int32, shape, 1) * row_factor
    )


def hash_rows(pattern_ref, out_ref, base, row, width):
    offset = base + (wrapped(row * col_factor) if isinstance(row, int) else row * col_factor)
    for first in range(0, width, sub_cols):
        last = min(first + sub_cols, width)
        out_ref[pl.ds(row, sub_rows), first:last] = to_gauss(pattern_ref[:, first:last] + offset)


def hash_tile(pattern_ref, out_ref, base):
    rows, width = out_ref.shape
    for row in range(0, rows, sub_rows):
        hash_rows(pattern_ref, out_ref, base, row, width)


def dot_nt(lhs, rhs):
    return lax.dot_general(
        lhs, rhs, (((1,), (1,)), ((), ())), preferred_element_type=jnp.float32
    )


def counter(source, which):
    if source.dtype == jnp.int32:
        return source[which]
    row = source[source.shape[0] - 16 :, 0:128].astype(jnp.float32)[0:1]
    lane = lax.broadcasted_iota(jnp.int32, row.shape, 1) - 3 * which
    zero = jnp.zeros_like(row)
    value = zero
    for digit in range(3):
        value += jnp.where(lane == digit, row * float(256**digit), zero)
    return jnp.sum(value).astype(jnp.int32)


def row_base(source, place, rows):
    return counter(source, 0) * stream_factor + place * wrapped(rows * row_factor)


def col_base(source, place, columns):
    return counter(source, 1) * stream_factor + place * wrapped(columns * row_factor)


def half():
    core = lax.rem(lax.axis_index("ex"), 2)
    return jnp.bitwise_xor(core, lax.shift_right_logical(lax.axis_index("param"), 1))


def first_dim(halves, dims):
    if halves == 1:
        return jnp.int32(0)
    return half() * wrapped(dims * col_factor)


def places(parts):
    place = lax.axis_index("param")
    if parts != 4:
        return place, place, jnp.int32(0), jnp.int32(0)
    early_at = 2 * jnp.bitwise_and(place, 1) + lax.shift_right_logical(place, 1)
    return place, jnp.bitwise_xor(place, 1), early_at, jnp.bitwise_xor(early_at, 1)


def rows_at(step, size):
    return pl.ds(pl.multiple_of(step * size, size), size)


def stream(steps, hash_at, use, beside_first):
    hash_at(0, 0)
    beside_first()

    def body(turn, carry):
        hash_at(2 * turn + 1, 1)
        use(2 * turn, 0)
        hash_at(2 * turn + 2, 0)
        use(2 * turn + 1, 1)
        return carry

    lax.fori_loop(0, steps // 2 - 1, body, 0)
    hash_at(steps - 1, 1)
    use(steps - 2, 0)
    use(steps - 1, 1)


def call(kernel, name, operands, outs, scratch, flops, megabytes):
    spaces = [pltpu.SMEM if array.dtype == jnp.int32 else pltpu.VMEM for array in operands]
    return pl.pallas_call(
        kernel,
        in_specs=[pl.BlockSpec(memory_space=space) for space in spaces],
        out_specs=[pl.BlockSpec(memory_space=pltpu.VMEM)] * len(outs),
        out_shape=outs,
        scratch_shapes=scratch,
        compiler_params=pltpu.CompilerParams(vmem_limit_bytes=megabytes * 2**20),
        cost_estimate=pl.CostEstimate(flops=flops, bytes_accessed=0, transcendentals=0),
        name=name,
    )(*operands)


def floats(*shape):
    return jax.ShapeDtypeStruct(shape, jnp.float32)


def digits_kernel(acts_ref, counters_ref, out_ref):
    tokens, rows = acts_ref.shape
    out_ref[:tokens, :] = acts_ref[...]
    lane = lax.broadcasted_iota(jnp.int32, (16, rows), 1)
    digits = jnp.zeros((16, rows), jnp.int32)
    for which in range(2):
        for digit in range(3):
            value = lax.shift_right_logical(counters_ref[which], jnp.int32(8 * digit))
            digits = jnp.where(lane == 3 * which + digit, jnp.bitwise_and(value, 255), digits)
    out_ref[tokens:, :] = digits.astype(jnp.float32).astype(out_ref.dtype)


def with_digits(acts, counters):
    tokens, rows = acts.shape
    (out,) = call(
        digits_kernel,
        "with_digits",
        [acts, counters],
        [jax.ShapeDtypeStruct((tokens + 16, rows), acts.dtype)],
        [],
        0,
        8,
    )
    return out


def ahead_kernel(parts, halves, kinds, sources, *refs):
    sources_in, outs, pattern_ref = refs[:sources], refs[sources:-1], refs[-1]
    _, partner, early_at, late_at = places(parts)
    dims, columns = outs[0].shape
    fill_pattern(pattern_ref)
    bases = []
    for kind, which in kinds:
        if kind == "row":
            base = row_base(sources_in[which], partner, columns)
        else:
            base = col_base(sources_in[which], early_at if kind == "early" else late_at, columns)
        bases.append(base + first_dim(halves, dims))

    def strip(number, carry):
        row = pl.multiple_of(number * sub_rows, sub_rows)
        for base, out_ref in zip(bases, outs):
            hash_rows(pattern_ref, out_ref, base, row, columns)
        return carry

    lax.fori_loop(0, dims // sub_rows, strip, 0, unroll=max(1, 4 // len(kinds)))


def ahead(parts, halves, kinds, sources, columns, dims):
    return call(
        functools.partial(ahead_kernel, parts, halves, kinds, len(sources)),
        "ahead",
        sources,
        [jax.ShapeDtypeStruct((dims, columns), jnp.bfloat16)] * len(kinds),
        [pltpu.VMEM((sub_rows, columns), jnp.int32)],
        1000 * dims * columns * len(kinds),
        8,
    )


def left_kernel(parts, halves, examples, source, *refs):
    acts = refs[:examples]
    u_ref, gram_ref, pattern_ref = refs[examples : examples + 3]
    tiles = refs[examples + 3 :]
    tokens, rows = acts[0].shape
    dims = u_ref.shape[0]
    fill_pattern(pattern_ref)
    base = row_base(source, places(parts)[0], rows) + first_dim(halves, dims)

    def hash_at(step, which):
        hash_tile(pattern_ref, tiles[which], base + step * wrapped(tile * col_factor))

    def grams():
        for e in range(examples):
            gram_ref[e] = dot_nt(acts[e][...], acts[e][...])

    def use(step, which):
        for e in range(examples):
            u_ref[rows_at(step, tile), e * tokens : (e + 1) * tokens] = dot_nt(
                tiles[which][...], acts[e][...]
            )

    stream(dims // tile, hash_at, use, grams)


def left(parts, halves, own, acts, dims):
    examples = len(acts)
    tokens, rows = acts[0].shape
    return call(
        functools.partial(left_kernel, parts, halves, examples),
        "left",
        [own, *acts],
        [floats(dims, examples * tokens), floats(examples, tokens, tokens)],
        [pltpu.VMEM((sub_rows, rows), jnp.int32)] + [pltpu.VMEM((tile, rows), jnp.bfloat16)] * 2,
        1000 * dims * rows,
        16,
    )


def middle_kernel(parts, halves, examples, source, u_ref, *refs):
    backs, refs = refs[:examples], refs[examples:]
    total_ref, gram_ref, pattern_ref = refs[:3]
    tiles = refs[3:]
    dims = total_ref.shape[0]
    tokens, columns = backs[0].shape
    fill_pattern(pattern_ref)
    base = col_base(source, places(parts)[2], columns) + first_dim(halves, dims)

    def hash_at(step, which):
        hash_tile(pattern_ref, tiles[which], base + step * wrapped(tile * col_factor))

    def grams():
        for e in range(examples):
            gram_ref[e] = dot_nt(backs[e][...], backs[e][...])

    def use(step, which):
        rows = rows_at(step, tile)
        for e in range(examples):
            here = slice(e * tokens, (e + 1) * tokens)
            total_ref[rows, here] = u_ref[rows, here] * dot_nt(tiles[which][...], backs[e][...])

    stream(dims // tile, hash_at, use, grams)


def middle(parts, halves, source, backs, u_own):
    examples = len(backs)
    tokens, columns = backs[0].shape
    dims = u_own.shape[0]
    return call(
        functools.partial(middle_kernel, parts, halves, examples),
        "middle",
        [source, u_own, *backs],
        [floats(dims, examples * tokens), floats(examples, tokens, tokens)],
        [pltpu.VMEM((sub_rows, columns), jnp.int32)]
        + [pltpu.VMEM((tile, columns), jnp.bfloat16)] * 2,
        1000 * dims * columns,
        20,
    )


def products_kernel(examples, u_own, row_other, col_own, col_other, *refs):
    acts, backs = refs[:examples], refs[examples : 2 * examples]
    total_ref, u_other, gram_a_ref, gram_b_ref = refs[2 * examples :]
    tokens = backs[0].shape[0]
    for e in range(examples):
        here = slice(e * tokens, (e + 1) * tokens)
        gram_b_ref[e] = dot_nt(backs[e][...], backs[e][...])
        for first in range(0, total_ref.shape[0], tile):
            rows = slice(first, first + tile)
            total_ref[rows, here] = u_own[rows, here] * dot_nt(col_own[rows, :], backs[e][...])
    for e in range(examples):
        here = slice(e * tokens, (e + 1) * tokens)
        gram_a_ref[e] = dot_nt(acts[e][:tokens, :], acts[e][:tokens, :])
        for first in range(0, total_ref.shape[0], tile):
            rows = slice(first, first + tile)
            u_piece = dot_nt(row_other[rows, :], acts[e][:tokens, :])
            u_other[rows, here] = u_piece
            total_ref[rows, here] += u_piece * dot_nt(col_other[rows, :], backs[e][...])


def products(u_own, row_other, cols, acts, backs):
    examples = len(backs)
    tokens = backs[0].shape[0]
    dims, lanes = u_own.shape
    gram = floats(examples, tokens, tokens)
    return call(
        functools.partial(products_kernel, examples),
        "products",
        [u_own, row_other, *cols, *acts, *backs],
        [floats(dims, lanes), floats(dims, lanes), gram, gram],
        [],
        4000 * dims * lanes,
        20,
    )


def late_kernel(parts, halves, examples, blocks, *refs):
    u_refs, refs = refs[:blocks], refs[blocks:]
    total_ref, refs = refs[0], refs[1:]
    sides = max(blocks, 1)
    grams_a, grams_b, refs = refs[:sides], refs[sides], refs[sides + 1 :]
    backs = ()
    if blocks:
        backs, refs = refs[:examples], refs[examples:]
        cols, refs = refs[:blocks], refs[blocks:]
    outs = refs
    tokens = grams_b.shape[1]
    dims = total_ref.shape[0]
    part_dims = outs[0].shape[1] - 128
    place = lax.axis_index("param")

    def send(e, number, columns, values):
        if halves == 1:
            slot = lax.rem(number - place + parts, parts)
        else:
            slot = 2 * jnp.bitwise_xor(number, jnp.bitwise_and(place, 1)) + e
        for which, out in enumerate(outs):

            @pl.when(slot == which)
            def _():
                out[:, columns] = values

    across = []
    for e in range(examples):
        here = slice(e * tokens, (e + 1) * tokens)
        for step in range(dims // tile):
            rows = slice(step * tile, (step + 1) * tile)
            total = total_ref[rows, here]
            for block in range(blocks):
                total += u_refs[block][rows, here] * dot_nt(cols[block][rows, :], backs[e][...])
            lane_sum = total[:, :128]
            for begin in range(128, tokens, 128):
                lane_sum += total[:, begin : begin + 128]
            across.append(jnp.sum(lane_sum.T, axis=0, keepdims=True))
    for e in range(examples):
        gram_a = grams_a[0][e]
        for more in grams_a[1:]:
            gram_a = gram_a + more[e]
        gram_b = grams_b[e]
        if blocks:
            gram_b = gram_b + dot_nt(backs[e][...], backs[e][...])
        both = jnp.full((1, 128), jnp.sum(gram_a * gram_b), jnp.float32)
        for number in range(parts // halves):
            send(e, number, slice(part_dims, part_dims + 128), both)
            step_dims = min(tile, part_dims)
            for begin in range(0, part_dims, step_dims):
                at = number * part_dims + begin
                step, inside = divmod(at, tile)
                values = across[e * (dims // tile) + step][:, inside : inside + step_dims]
                send(e, number, slice(begin, begin + step_dims), values)


def late(parts, halves, us, total, grams, backs, cols):
    blocks = len(cols)
    dims, lanes = total.shape
    examples, tokens = grams[0].shape[:2]
    message = jax.ShapeDtypeStruct((1, dims * halves // parts + 128), jnp.float32)
    return call(
        functools.partial(late_kernel, parts, halves, examples, blocks),
        "late",
        [*us[:blocks], total, *grams, *backs, *cols],
        [message] * parts,
        [],
        2 * blocks * dims * lanes * 1024,
        24,
    )


def on_device(parts, group, activations, backprops, block_counters):
    tokens, columns = backprops.shape[1:]
    counters = block_counters.reshape(2)
    acts = activations[0]
    backs = backprops[0]
    if parts == 4 and group % 2 == 0:
        swap = [(0, 1), (1, 0), (2, 3), (3, 2)]
        halves = 2
        dims = K // halves

        def with_sibling(array):
            pairs = [(device, device ^ 1) for device in range(group)]
            return [array, lax.ppermute(array, "ex", pairs)]

        other_acts = lax.ppermute(with_digits(acts, counters), "param", swap)
        early_backs = lax.ppermute(backs, "param", [(0, 0), (1, 2), (2, 1), (3, 3)])
        own_pair = with_sibling(acts)
        late_backs = lax.ppermute(backs, "param", [(0, 2), (3, 1), (1, 0), (2, 3)])
        (late_own,) = ahead(parts, halves, [("late", 0)], [counters], columns, dims)
        u_own, gram_own = left(parts, halves, counters, own_pair, dims)
        other_acts, u_own, late_own = lax.optimization_barrier((other_acts, u_own, late_own))
        made = ahead(
            parts,
            halves,
            [("early", 0), ("early", 1), ("late", 1), ("row", 1)],
            [counters, other_acts],
            columns,
            dims,
        )
        other_acts, early_backs, late_backs, made = lax.optimization_barrier(
            (other_acts, early_backs, late_backs, made)
        )
        early_pair = with_sibling(early_backs)
        other_pair = with_sibling(other_acts)
        late_pair = with_sibling(late_backs)
        *early_cols, late_other, row_other = made
        total, u_other, gram_other, gram_early = products(
            u_own, row_other, early_cols, other_pair, early_pair
        )
        messages = late(
            parts,
            halves,
            [u_own, u_other],
            total,
            [gram_own, gram_other, gram_early],
            late_pair,
            [late_own, late_other],
        )
    else:
        halves = 1
        every_back = lax.all_gather(backs, "param", axis=1, tiled=True)
        u_own, gram_own = left(parts, halves, counters, [acts], K)
        total, gram_backs = middle(parts, halves, counters, [every_back], u_own)
        messages = late(parts, halves, [], total, [gram_own, gram_backs], [], [])
    summed = None
    for number, message in enumerate(messages):
        if halves == 1:
            moves = [(source, (source + number) % parts) for source in range(parts)]
            moved = lax.ppermute(message, "param", moves) if number else message
        else:
            moves = [
                (
                    z * group + chip * 2 + core,
                    (2 * (core ^ z // 2) + (z % 2 ^ number // 2)) * group
                    + chip * 2
                    + (core ^ number % 2),
                )
                for z in range(parts)
                for chip in range(group // 2)
                for core in range(2)
            ]
            moved = lax.ppermute(message, ("param", "ex"), moves)
        summed = moved if summed is None else summed + moved
    part_dims = K // parts
    sumsq = jnp.maximum(summed[:, part_dims], 0.0)
    features = summed[:, :part_dims] * (lax.rsqrt(sumsq + epsilon) * unscale)[:, None]
    return (features, jnp.sqrt(sumsq))


def solution(mesh):
    return jax.shard_map(
        functools.partial(on_device, mesh.shape["param"], mesh.shape["ex"]),
        mesh=mesh,
        in_specs=(
            P(("grp", "ex"), None, "param"),
            P(("grp", "ex"), None, "param"),
            P(None, "param"),
        ),
        out_specs=(P(("grp", "ex"), "param"), P(("grp", "ex"))),
        check_vma=False,
    )
```

```python
import functools

import jax
import jax.numpy as jnp
from jax import lax
from jax.experimental import pallas as pl
from jax.experimental.pallas import tpu as pltpu
from jax.sharding import PartitionSpec as P

K = 2048

mix_factor = 73244475
stream_factor = 668265261
row_factor = 374761393
col_factor = 1103515245
epsilon = 1e-06
unscale = 1.0 / (128.0 * 128.0)

tile = 256
sub_rows = 16
sub_cols = 256


def wrapped(number):
    return jnp.int32((number + 2**31) % 2**32 - 2**31)


def scramble(hashed):
    sixteen = jnp.int32(16)
    hashed = jnp.bitwise_xor(hashed, lax.shift_right_logical(hashed, sixteen))
    hashed = hashed * mix_factor
    hashed = jnp.bitwise_xor(hashed, lax.shift_right_logical(hashed, sixteen))
    hashed = hashed * mix_factor
    return jnp.bitwise_xor(hashed, lax.shift_right_logical(hashed, sixteen))


def to_gauss(hashed):
    hashed = scramble(hashed)
    pairs = jnp.int32(0x00FF00FF)
    two_sums = jnp.bitwise_and(hashed, pairs) + jnp.bitwise_and(
        lax.shift_right_logical(hashed, jnp.int32(8)), pairs
    )
    total = lax.shift_right_logical(two_sums * jnp.int32(0x10001), jnp.int32(16))
    return (total - 510).astype(jnp.float32).astype(jnp.bfloat16)


def fill_pattern(pattern_ref):
    shape = pattern_ref.shape
    pattern_ref[...] = (
        lax.broadcasted_iota(jnp.int32, shape, 0) * col_factor
        + lax.broadcasted_iota(jnp.int32, shape, 1) * row_factor
    )


def hash_rows(pattern_ref, out_ref, base, row, width):
    offset = base + (wrapped(row * col_factor) if isinstance(row, int) else row * col_factor)
    for first in range(0, width, sub_cols):
        last = min(first + sub_cols, width)
        out_ref[pl.ds(row, sub_rows), first:last] = to_gauss(pattern_ref[:, first:last] + offset)


def hash_tile(pattern_ref, out_ref, base):
    rows, width = out_ref.shape
    for row in range(0, rows, sub_rows):
        hash_rows(pattern_ref, out_ref, base, row, width)


def dot_nt(lhs, rhs):
    return lax.dot_general(
        lhs, rhs, (((1,), (1,)), ((), ())), preferred_element_type=jnp.float32
    )


def counter(source, which):
    if source.dtype == jnp.int32:
        return source[which]
    row = source[source.shape[0] - 16 :, 0:128].astype(jnp.float32)[0:1]
    lane = lax.broadcasted_iota(jnp.int32, row.shape, 1) - 3 * which
    zero = jnp.zeros_like(row)
    value = zero
    for digit in range(3):
        value += jnp.where(lane == digit, row * float(256**digit), zero)
    return jnp.sum(value).astype(jnp.int32)


def row_base(source, place, rows):
    return counter(source, 0) * stream_factor + place * wrapped(rows * row_factor)


def col_base(source, place, columns):
    return counter(source, 1) * stream_factor + place * wrapped(columns * row_factor)


def half():
    core = lax.rem(lax.axis_index("ex"), 2)
    return jnp.bitwise_xor(core, lax.shift_right_logical(lax.axis_index("param"), 1))


def first_dim(halves, dims):
    if halves == 1:
        return jnp.int32(0)
    return half() * wrapped(dims * col_factor)


def places(parts):
    place = lax.axis_index("param")
    if parts != 4:
        return place, place, jnp.int32(0), jnp.int32(0)
    early_at = 2 * jnp.bitwise_and(place, 1) + lax.shift_right_logical(place, 1)
    return place, jnp.bitwise_xor(place, 1), early_at, jnp.bitwise_xor(early_at, 1)


def rows_at(step, size):
    return pl.ds(pl.multiple_of(step * size, size), size)


def stream(steps, hash_at, use, beside_first):
    hash_at(0, 0)
    beside_first()

    def body(turn, carry):
        hash_at(2 * turn + 1, 1)
        use(2 * turn, 0)
        hash_at(2 * turn + 2, 0)
        use(2 * turn + 1, 1)
        return carry

    lax.fori_loop(0, steps // 2 - 1, body, 0)
    hash_at(steps - 1, 1)
    use(steps - 2, 0)
    use(steps - 1, 1)


def call(kernel, name, operands, outs, scratch, flops, megabytes):
    spaces = [pltpu.SMEM if array.dtype == jnp.int32 else pltpu.VMEM for array in operands]
    return pl.pallas_call(
        kernel,
        in_specs=[pl.BlockSpec(memory_space=space) for space in spaces],
        out_specs=[pl.BlockSpec(memory_space=pltpu.VMEM)] * len(outs),
        out_shape=outs,
        scratch_shapes=scratch,
        compiler_params=pltpu.CompilerParams(vmem_limit_bytes=megabytes * 2**20),
        cost_estimate=pl.CostEstimate(flops=flops, bytes_accessed=0, transcendentals=0),
        name=name,
    )(*operands)


def floats(*shape):
    return jax.ShapeDtypeStruct(shape, jnp.float32)


def digits_kernel(acts_ref, counters_ref, out_ref):
    tokens, rows = acts_ref.shape
    out_ref[:tokens, :] = acts_ref[...]
    lane = lax.broadcasted_iota(jnp.int32, (16, rows), 1)
    digits = jnp.zeros((16, rows), jnp.int32)
    for which in range(2):
        for digit in range(3):
            value = lax.shift_right_logical(counters_ref[which], jnp.int32(8 * digit))
            digits = jnp.where(lane == 3 * which + digit, jnp.bitwise_and(value, 255), digits)
    out_ref[tokens:, :] = digits.astype(jnp.float32).astype(out_ref.dtype)


def with_digits(acts, counters):
    tokens, rows = acts.shape
    (out,) = call(
        digits_kernel,
        "with_digits",
        [acts, counters],
        [jax.ShapeDtypeStruct((tokens + 16, rows), acts.dtype)],
        [],
        0,
        8,
    )
    return out


def ahead_kernel(parts, halves, kinds, sources, *refs):
    sources_in, outs, pattern_ref = refs[:sources], refs[sources:-1], refs[-1]
    _, partner, early_at, late_at = places(parts)
    dims, columns = outs[0].shape
    fill_pattern(pattern_ref)
    bases = []
    for kind, which in kinds:
        if kind == "row":
            base = row_base(sources_in[which], partner, columns)
        else:
            base = col_base(sources_in[which], early_at if kind == "early" else late_at, columns)
        bases.append(base + first_dim(halves, dims))

    def strip(number, carry):
        row = pl.multiple_of(number * sub_rows, sub_rows)
        for base, out_ref in zip(bases, outs):
            hash_rows(pattern_ref, out_ref, base, row, columns)
        return carry

    lax.fori_loop(0, dims // sub_rows, strip, 0, unroll=max(1, 4 // len(kinds)))


def ahead(parts, halves, kinds, sources, columns, dims):
    return call(
        functools.partial(ahead_kernel, parts, halves, kinds, len(sources)),
        "ahead",
        sources,
        [jax.ShapeDtypeStruct((dims, columns), jnp.bfloat16)] * len(kinds),
        [pltpu.VMEM((sub_rows, columns), jnp.int32)],
        1000 * dims * columns * len(kinds),
        8,
    )


def left_kernel(parts, halves, examples, source, *refs):
    acts = refs[:examples]
    u_ref, gram_ref, pattern_ref = refs[examples : examples + 3]
    tiles = refs[examples + 3 :]
    tokens, rows = acts[0].shape
    dims = u_ref.shape[0]
    fill_pattern(pattern_ref)
    base = row_base(source, places(parts)[0], rows) + first_dim(halves, dims)

    def hash_at(step, which):
        hash_tile(pattern_ref, tiles[which], base + step * wrapped(tile * col_factor))

    def grams():
        for e in range(examples):
            gram_ref[e] = dot_nt(acts[e][...], acts[e][...])

    def use(step, which):
        for e in range(examples):
            u_ref[rows_at(step, tile), e * tokens : (e + 1) * tokens] = dot_nt(
                tiles[which][...], acts[e][...]
            )

    stream(dims // tile, hash_at, use, grams)


def left(parts, halves, own, acts, dims):
    examples = len(acts)
    tokens, rows = acts[0].shape
    return call(
        functools.partial(left_kernel, parts, halves, examples),
        "left",
        [own, *acts],
        [floats(dims, examples * tokens), floats(examples, tokens, tokens)],
        [pltpu.VMEM((sub_rows, rows), jnp.int32)] + [pltpu.VMEM((tile, rows), jnp.bfloat16)] * 2,
        1000 * dims * rows,
        16,
    )


def middle_kernel(parts, halves, examples, source, u_ref, *refs):
    backs, refs = refs[:examples], refs[examples:]
    total_ref, gram_ref, pattern_ref = refs[:3]
    tiles = refs[3:]
    dims = total_ref.shape[0]
    tokens, columns = backs[0].shape
    fill_pattern(pattern_ref)
    base = col_base(source, places(parts)[2], columns) + first_dim(halves, dims)

    def hash_at(step, which):
        hash_tile(pattern_ref, tiles[which], base + step * wrapped(tile * col_factor))

    def grams():
        for e in range(examples):
            gram_ref[e] = dot_nt(backs[e][...], backs[e][...])

    def use(step, which):
        rows = rows_at(step, tile)
        for e in range(examples):
            here = slice(e * tokens, (e + 1) * tokens)
            total_ref[rows, here] = u_ref[rows, here] * dot_nt(tiles[which][...], backs[e][...])

    stream(dims // tile, hash_at, use, grams)


def middle(parts, halves, source, backs, u_own):
    examples = len(backs)
    tokens, columns = backs[0].shape
    dims = u_own.shape[0]
    return call(
        functools.partial(middle_kernel, parts, halves, examples),
        "middle",
        [source, u_own, *backs],
        [floats(dims, examples * tokens), floats(examples, tokens, tokens)],
        [pltpu.VMEM((sub_rows, columns), jnp.int32)]
        + [pltpu.VMEM((tile, columns), jnp.bfloat16)] * 2,
        1000 * dims * columns,
        20,
    )


def example_kernel(which, *refs):
    u_own, row_other, early_own, early_other, late_own, late_other = refs[:6]
    acts, early_backs, late_backs, gram_own = refs[6:10]
    outs = refs[10:]
    tokens = early_backs.shape[0]
    dims = row_other.shape[0]
    part_dims = outs[0].shape[1] - 128
    here = slice(which * tokens, (which + 1) * tokens)
    across = []
    for first in range(0, dims, tile):
        rows = slice(first, first + tile)
        right_own = dot_nt(early_own[rows, :], early_backs[...])
        right_own += dot_nt(late_own[rows, :], late_backs[...])
        right_other = dot_nt(early_other[rows, :], early_backs[...])
        right_other += dot_nt(late_other[rows, :], late_backs[...])
        u_other = dot_nt(row_other[rows, :], acts[:tokens, :])
        total = u_own[rows, here] * right_own + u_other * right_other
        lane_sum = total[:, :128]
        for begin in range(128, tokens, 128):
            lane_sum += total[:, begin : begin + 128]
        across.append(jnp.sum(lane_sum.T, axis=0, keepdims=True))
    gram_a = gram_own[which] + dot_nt(acts[:tokens, :], acts[:tokens, :])
    gram_b = dot_nt(early_backs[...], early_backs[...]) + dot_nt(late_backs[...], late_backs[...])
    both = jnp.full((1, 128), jnp.sum(gram_a * gram_b), jnp.float32)
    low = jnp.bitwise_and(lax.axis_index("param"), 1)
    for number in range(len(outs)):
        slot = jnp.bitwise_xor(number, low)
        for at, out in enumerate(outs):

            @pl.when(slot == at)
            def _():
                out[:, part_dims:] = both
                for begin in range(0, part_dims, tile):
                    step = (number * part_dims + begin) // tile
                    out[:, begin : begin + tile] = across[step]


def one_example(which, u_own, made, acts, early_backs, late_backs, gram_own, parts):
    dims = made[0].shape[0]
    early_own, early_other, late_own, late_other, row_other = made
    return call(
        functools.partial(example_kernel, which),
        "one_example",
        [u_own, row_other, early_own, early_other, late_own, late_other]
        + [acts, early_backs, late_backs, gram_own],
        [floats(1, dims * 2 // parts + 128)] * 2,
        [],
        4 * 10**9,
        24,
    )


def sums_kernel(parts, examples, total_ref, gram_a_ref, gram_b_ref, *outs):
    tokens = gram_b_ref.shape[1]
    dims = total_ref.shape[0]
    part_dims = outs[0].shape[1] - 128
    place = lax.axis_index("param")

    def send(number, columns, values):
        slot = lax.rem(number - place + parts, parts)
        for which, out in enumerate(outs):

            @pl.when(slot == which)
            def _():
                out[:, columns] = values

    across = []
    for step in range(dims // tile):
        total = total_ref[step * tile : (step + 1) * tile, :]
        lane_sum = total[:, :128]
        for begin in range(128, tokens, 128):
            lane_sum += total[:, begin : begin + 128]
        across.append(jnp.sum(lane_sum.T, axis=0, keepdims=True))
    both = jnp.full((1, 128), jnp.sum(gram_a_ref[0] * gram_b_ref[0]), jnp.float32)
    step_dims = min(tile, part_dims)
    for number in range(parts):
        send(number, slice(part_dims, part_dims + 128), both)
        for begin in range(0, part_dims, step_dims):
            step, inside = divmod(number * part_dims + begin, tile)
            send(number, slice(begin, begin + step_dims), across[step][:, inside : inside + step_dims])


def sums(parts, total, gram_a, gram_b):
    message = floats(1, total.shape[0] // parts + 128)
    return call(
        functools.partial(sums_kernel, parts, 1),
        "sums",
        [total, gram_a, gram_b],
        [message] * parts,
        [],
        10**9,
        16,
    )


def finish_kernel(*refs):
    messages, (features_ref, norm_ref) = refs[:-2], refs[-2:]
    part_dims = features_ref.shape[1]
    summed = messages[0][...]
    for message in messages[1:]:
        summed += message[...]
    sumsq = jnp.maximum(summed[:, part_dims : part_dims + 128], 0.0)
    scale = lax.rsqrt(sumsq + epsilon) * unscale
    for begin in range(0, part_dims, 128):
        width = min(128, part_dims - begin)
        features_ref[:, begin : begin + width] = summed[:, begin : begin + width] * scale[:, :width]
    norm_ref[0] = jnp.max(jnp.sqrt(sumsq))


def finish(messages, part_dims):
    return pl.pallas_call(
        finish_kernel,
        in_specs=[pl.BlockSpec(memory_space=pltpu.VMEM)] * len(messages),
        out_specs=[pl.BlockSpec(memory_space=space) for space in (pltpu.VMEM, pltpu.SMEM)],
        out_shape=[floats(1, part_dims), floats(1)],
        compiler_params=pltpu.CompilerParams(vmem_limit_bytes=4 * 2**20),
        name="finish",
    )(*messages)


def on_device(parts, group, activations, backprops, block_counters):
    tokens, columns = backprops.shape[1:]
    counters = block_counters.reshape(2)
    acts = activations[0]
    backs = backprops[0]
    if parts == 4 and group % 2 == 0:
        swap = [(0, 1), (1, 0), (2, 3), (3, 2)]
        halves = 2
        dims = K // halves

        def with_sibling(array):
            pairs = [(device, device ^ 1) for device in range(group)]
            return [array, lax.ppermute(array, "ex", pairs)]

        other_acts = lax.ppermute(with_digits(acts, counters), "param", swap)
        early_backs = lax.ppermute(backs, "param", [(0, 0), (1, 2), (2, 1), (3, 3)])
        own_pair = with_sibling(acts)
        late_backs = lax.ppermute(backs, "param", [(0, 2), (3, 1), (1, 0), (2, 3)])
        (late_own,) = ahead(parts, halves, [("late", 0)], [counters], columns, dims)
        u_own, gram_own = left(parts, halves, counters, own_pair, dims)
        other_acts, u_own, late_own = lax.optimization_barrier((other_acts, u_own, late_own))
        made = ahead(
            parts,
            halves,
            [("early", 0), ("early", 1), ("late", 1), ("row", 1)],
            [counters, other_acts],
            columns,
            dims,
        )
        other_acts, early_backs, late_backs, made = lax.optimization_barrier(
            (other_acts, early_backs, late_backs, made)
        )
        early_pair = with_sibling(early_backs)
        other_pair = with_sibling(other_acts)
        late_pair = with_sibling(late_backs)
        early_own, early_other, late_other, row_other = made
        made = [early_own, early_other, late_own, late_other, row_other]
        messages = [None] * parts
        for which in range(2):
            messages[which], messages[2 + which] = one_example(
                which,
                u_own,
                made,
                other_pair[which],
                early_pair[which],
                late_pair[which],
                gram_own,
                parts,
            )
        messages = lax.optimization_barrier(messages)
    else:
        halves = 1
        every_back = lax.all_gather(backs, "param", axis=1, tiled=True)
        u_own, gram_own = left(parts, halves, counters, [acts], K)
        total, gram_backs = middle(parts, halves, counters, [every_back], u_own)
        messages = sums(parts, total, gram_own, gram_backs)
    received = []
    for number, message in enumerate(messages):
        if halves == 1:
            moves = [(source, (source + number) % parts) for source in range(parts)]
            received.append(lax.ppermute(message, "param", moves) if number else message)
        else:
            moves = [
                (
                    z * group + chip * 2 + core,
                    (2 * (core ^ z // 2) + (z % 2 ^ number // 2)) * group
                    + chip * 2
                    + (core ^ number % 2),
                )
                for z in range(parts)
                for chip in range(group // 2)
                for core in range(2)
            ]
            received.append(lax.ppermute(message, ("param", "ex"), moves))
    features, norm = finish(received, K // parts)
    return (features, norm)


def solution(mesh):
    return jax.shard_map(
        functools.partial(on_device, mesh.shape["param"], mesh.shape["ex"]),
        mesh=mesh,
        in_specs=(
            P(("grp", "ex"), None, "param"),
            P(("grp", "ex"), None, "param"),
            P(None, "param"),
        ),
        out_specs=(P(("grp", "ex"), "param"), P(("grp", "ex"))),
        check_vma=False,
    )
```

```python
import functools

import jax
import jax.numpy as jnp
from jax import lax
from jax.experimental import pallas as pl
from jax.experimental.pallas import tpu as pltpu
from jax.sharding import PartitionSpec as P

K = 2048

mix_factor = 73244475
stream_factor = 668265261
row_factor = 374761393
col_factor = 1103515245
epsilon = 1e-06
unscale = 1.0 / (128.0 * 128.0)

tile = 256
sub_rows = 16
sub_cols = 256


def wrapped(number):
    return jnp.int32((number + 2**31) % 2**32 - 2**31)


def scramble(hashed):
    sixteen = jnp.int32(16)
    hashed = jnp.bitwise_xor(hashed, lax.shift_right_logical(hashed, sixteen))
    hashed = hashed * mix_factor
    hashed = jnp.bitwise_xor(hashed, lax.shift_right_logical(hashed, sixteen))
    hashed = hashed * mix_factor
    return jnp.bitwise_xor(hashed, lax.shift_right_logical(hashed, sixteen))


def to_gauss(hashed):
    hashed = scramble(hashed)
    pairs = jnp.int32(0x00FF00FF)
    two_sums = jnp.bitwise_and(hashed, pairs) + jnp.bitwise_and(
        lax.shift_right_logical(hashed, jnp.int32(8)), pairs
    )
    total = lax.shift_right_logical(two_sums * jnp.int32(0x10001), jnp.int32(16))
    return (total - 510).astype(jnp.float32).astype(jnp.bfloat16)


def fill_pattern(pattern_ref):
    shape = pattern_ref.shape
    pattern_ref[...] = (
        lax.broadcasted_iota(jnp.int32, shape, 0) * col_factor
        + lax.broadcasted_iota(jnp.int32, shape, 1) * row_factor
    )


def hash_rows(pattern_ref, out_ref, base, row, width):
    offset = base + (wrapped(row * col_factor) if isinstance(row, int) else row * col_factor)
    for first in range(0, width, sub_cols):
        last = min(first + sub_cols, width)
        out_ref[pl.ds(row, sub_rows), first:last] = to_gauss(pattern_ref[:, first:last] + offset)


def hash_tile(pattern_ref, out_ref, base):
    rows, width = out_ref.shape
    for row in range(0, rows, sub_rows):
        hash_rows(pattern_ref, out_ref, base, row, width)


def dot_nt(lhs, rhs):
    return lax.dot_general(
        lhs, rhs, (((1,), (1,)), ((), ())), preferred_element_type=jnp.float32
    )


def counter(source, which):
    if source.dtype == jnp.int32:
        return source[which]
    row = source[source.shape[0] - 16 :, 0:128].astype(jnp.float32)[0:1]
    lane = lax.broadcasted_iota(jnp.int32, row.shape, 1) - 3 * which
    zero = jnp.zeros_like(row)
    value = zero
    for digit in range(3):
        value += jnp.where(lane == digit, row * float(256**digit), zero)
    return jnp.sum(value).astype(jnp.int32)


def row_base(source, place, rows):
    return counter(source, 0) * stream_factor + place * wrapped(rows * row_factor)


def col_base(source, place, columns):
    return counter(source, 1) * stream_factor + place * wrapped(columns * row_factor)


def half():
    core = lax.rem(lax.axis_index("ex"), 2)
    return jnp.bitwise_xor(core, lax.shift_right_logical(lax.axis_index("param"), 1))


def first_dim(halves, dims):
    if halves == 1:
        return jnp.int32(0)
    return half() * wrapped(dims * col_factor)


def places(parts):
    place = lax.axis_index("param")
    if parts != 4:
        return place, place, jnp.int32(0), jnp.int32(0)
    early_at = 2 * jnp.bitwise_and(place, 1) + lax.shift_right_logical(place, 1)
    return place, jnp.bitwise_xor(place, 1), early_at, jnp.bitwise_xor(early_at, 1)


def rows_at(step, size):
    return pl.ds(pl.multiple_of(step * size, size), size)


def stream(steps, hash_at, use, beside_first):
    hash_at(0, 0)
    beside_first()

    def body(turn, carry):
        hash_at(2 * turn + 1, 1)
        use(2 * turn, 0)
        hash_at(2 * turn + 2, 0)
        use(2 * turn + 1, 1)
        return carry

    lax.fori_loop(0, steps // 2 - 1, body, 0)
    hash_at(steps - 1, 1)
    use(steps - 2, 0)
    use(steps - 1, 1)


def call(kernel, name, operands, outs, scratch, flops, megabytes):
    spaces = [pltpu.SMEM if array.dtype == jnp.int32 else pltpu.VMEM for array in operands]
    return pl.pallas_call(
        kernel,
        in_specs=[pl.BlockSpec(memory_space=space) for space in spaces],
        out_specs=[pl.BlockSpec(memory_space=pltpu.VMEM)] * len(outs),
        out_shape=outs,
        scratch_shapes=scratch,
        compiler_params=pltpu.CompilerParams(vmem_limit_bytes=megabytes * 2**20),
        cost_estimate=pl.CostEstimate(flops=flops, bytes_accessed=0, transcendentals=0),
        name=name,
    )(*operands)


def floats(*shape):
    return jax.ShapeDtypeStruct(shape, jnp.float32)


def digits_kernel(acts_ref, counters_ref, out_ref):
    tokens, rows = acts_ref.shape
    out_ref[:tokens, :] = acts_ref[...]
    lane = lax.broadcasted_iota(jnp.int32, (16, rows), 1)
    digits = jnp.zeros((16, rows), jnp.int32)
    for which in range(2):
        for digit in range(3):
            value = lax.shift_right_logical(counters_ref[which], jnp.int32(8 * digit))
            digits = jnp.where(lane == 3 * which + digit, jnp.bitwise_and(value, 255), digits)
    out_ref[tokens:, :] = digits.astype(jnp.float32).astype(out_ref.dtype)


def with_digits(acts, counters):
    tokens, rows = acts.shape
    (out,) = call(
        digits_kernel,
        "with_digits",
        [acts, counters],
        [jax.ShapeDtypeStruct((tokens + 16, rows), acts.dtype)],
        [],
        0,
        8,
    )
    return out


def ahead_kernel(parts, halves, kinds, sources, *refs):
    sources_in, outs, pattern_ref = refs[:sources], refs[sources:-1], refs[-1]
    _, partner, early_at, late_at = places(parts)
    dims, columns = outs[0].shape
    fill_pattern(pattern_ref)
    bases = []
    for kind, which in kinds:
        if kind == "row":
            base = row_base(sources_in[which], partner, columns)
        else:
            base = col_base(sources_in[which], early_at if kind == "early" else late_at, columns)
        bases.append(base + first_dim(halves, dims))

    def strip(number, carry):
        row = pl.multiple_of(number * sub_rows, sub_rows)
        for base, out_ref in zip(bases, outs):
            hash_rows(pattern_ref, out_ref, base, row, columns)
        return carry

    lax.fori_loop(0, dims // sub_rows, strip, 0, unroll=max(1, 4 // len(kinds)))


def ahead(parts, halves, kinds, sources, columns, dims):
    return call(
        functools.partial(ahead_kernel, parts, halves, kinds, len(sources)),
        "ahead",
        sources,
        [jax.ShapeDtypeStruct((dims, columns), jnp.bfloat16)] * len(kinds),
        [pltpu.VMEM((sub_rows, columns), jnp.int32)],
        1000 * dims * columns * len(kinds),
        8,
    )


def left_kernel(parts, halves, examples, source, *refs):
    acts = refs[:examples]
    u_ref, gram_ref, pattern_ref = refs[examples : examples + 3]
    tiles = refs[examples + 3 :]
    tokens, rows = acts[0].shape
    dims = u_ref.shape[0]
    fill_pattern(pattern_ref)
    base = row_base(source, places(parts)[0], rows) + first_dim(halves, dims)

    def hash_at(step, which):
        hash_tile(pattern_ref, tiles[which], base + step * wrapped(tile * col_factor))

    def grams():
        for e in range(examples):
            gram_ref[e] = dot_nt(acts[e][...], acts[e][...])

    def use(step, which):
        for e in range(examples):
            u_ref[rows_at(step, tile), e * tokens : (e + 1) * tokens] = dot_nt(
                tiles[which][...], acts[e][...]
            )

    stream(dims // tile, hash_at, use, grams)


def left(parts, halves, own, acts, dims):
    examples = len(acts)
    tokens, rows = acts[0].shape
    return call(
        functools.partial(left_kernel, parts, halves, examples),
        "left",
        [own, *acts],
        [floats(dims, examples * tokens), floats(examples, tokens, tokens)],
        [pltpu.VMEM((sub_rows, rows), jnp.int32)] + [pltpu.VMEM((tile, rows), jnp.bfloat16)] * 2,
        1000 * dims * rows,
        16,
    )


def middle_kernel(parts, halves, examples, source, u_ref, *refs):
    backs, refs = refs[:examples], refs[examples:]
    total_ref, gram_ref, pattern_ref = refs[:3]
    tiles = refs[3:]
    dims = total_ref.shape[0]
    tokens, columns = backs[0].shape
    fill_pattern(pattern_ref)
    base = col_base(source, places(parts)[2], columns) + first_dim(halves, dims)

    def hash_at(step, which):
        hash_tile(pattern_ref, tiles[which], base + step * wrapped(tile * col_factor))

    def grams():
        for e in range(examples):
            gram_ref[e] = dot_nt(backs[e][...], backs[e][...])

    def use(step, which):
        rows = rows_at(step, tile)
        for e in range(examples):
            here = slice(e * tokens, (e + 1) * tokens)
            total_ref[rows, here] = u_ref[rows, here] * dot_nt(tiles[which][...], backs[e][...])

    stream(dims // tile, hash_at, use, grams)


def middle(parts, halves, source, backs, u_own):
    examples = len(backs)
    tokens, columns = backs[0].shape
    dims = u_own.shape[0]
    return call(
        functools.partial(middle_kernel, parts, halves, examples),
        "middle",
        [source, u_own, *backs],
        [floats(dims, examples * tokens), floats(examples, tokens, tokens)],
        [pltpu.VMEM((sub_rows, columns), jnp.int32)]
        + [pltpu.VMEM((tile, columns), jnp.bfloat16)] * 2,
        1000 * dims * columns,
        20,
    )


def partner_kernel(row_other, acts, u_ref, gram_ref):
    tokens = u_ref.shape[1]
    for first in range(0, u_ref.shape[0], tile):
        rows = slice(first, first + tile)
        u_ref[rows, :] = dot_nt(row_other[rows, :], acts[:tokens, :])
    gram_ref[...] = dot_nt(acts[:tokens, :], acts[:tokens, :])


def partner_left(row_other, acts, tokens):
    dims = row_other.shape[0]
    return call(
        partner_kernel,
        "partner_left",
        [row_other, acts],
        [floats(dims, tokens), floats(tokens, tokens)],
        [],
        10**9,
        12,
    )


def example_kernel(which, *refs):
    u_own, early_own, early_other, late_own, late_other = refs[:5]
    first_other, second_other, early_backs, late_backs, gram_own = refs[5:10]
    outs = refs[10:]
    tokens = early_backs.shape[0]
    dims = early_own.shape[0]
    part_dims = outs[0].shape[1] - 128
    here = slice(which * tokens, (which + 1) * tokens)
    across = []
    for first in range(0, dims, tile):
        rows = slice(first, first + tile)
        right_own = dot_nt(early_own[rows, :], early_backs[...])
        right_own += dot_nt(late_own[rows, :], late_backs[...])
        right_other = dot_nt(early_other[rows, :], early_backs[...])
        right_other += dot_nt(late_other[rows, :], late_backs[...])
        if which:
            u_other = dot_nt(first_other[rows, :], second_other[:tokens, :])
        else:
            u_other = first_other[rows, :]
        total = u_own[rows, here] * right_own + u_other * right_other
        lane_sum = total[:, :128]
        for begin in range(128, tokens, 128):
            lane_sum += total[:, begin : begin + 128]
        across.append(jnp.sum(lane_sum.T, axis=0, keepdims=True))
    if which:
        gram_a = gram_own[which] + dot_nt(second_other[:tokens, :], second_other[:tokens, :])
    else:
        gram_a = gram_own[which] + second_other[...]
    gram_b = dot_nt(early_backs[...], early_backs[...]) + dot_nt(late_backs[...], late_backs[...])
    both = jnp.full((1, 128), jnp.sum(gram_a * gram_b), jnp.float32)
    low = jnp.bitwise_and(lax.axis_index("param"), 1)
    for number in range(len(outs)):
        slot = jnp.bitwise_xor(number, low)
        for at, out in enumerate(outs):

            @pl.when(slot == at)
            def _():
                out[:, part_dims:] = both
                for begin in range(0, part_dims, tile):
                    step = (number * part_dims + begin) // tile
                    out[:, begin : begin + tile] = across[step]


def one_example(which, u_own, cols, other, early_backs, late_backs, gram_own, parts):
    dims = cols[0].shape[0]
    return call(
        functools.partial(example_kernel, which),
        "one_example",
        [u_own, *cols, *other, early_backs, late_backs, gram_own],
        [floats(1, dims * 2 // parts + 128)] * 2,
        [],
        4 * 10**9,
        24,
    )


def sums_kernel(parts, examples, total_ref, gram_a_ref, gram_b_ref, *outs):
    tokens = gram_b_ref.shape[1]
    dims = total_ref.shape[0]
    part_dims = outs[0].shape[1] - 128
    place = lax.axis_index("param")

    def send(number, columns, values):
        slot = lax.rem(number - place + parts, parts)
        for which, out in enumerate(outs):

            @pl.when(slot == which)
            def _():
                out[:, columns] = values

    across = []
    for step in range(dims // tile):
        total = total_ref[step * tile : (step + 1) * tile, :]
        lane_sum = total[:, :128]
        for begin in range(128, tokens, 128):
            lane_sum += total[:, begin : begin + 128]
        across.append(jnp.sum(lane_sum.T, axis=0, keepdims=True))
    both = jnp.full((1, 128), jnp.sum(gram_a_ref[0] * gram_b_ref[0]), jnp.float32)
    step_dims = min(tile, part_dims)
    for number in range(parts):
        send(number, slice(part_dims, part_dims + 128), both)
        for begin in range(0, part_dims, step_dims):
            step, inside = divmod(number * part_dims + begin, tile)
            send(number, slice(begin, begin + step_dims), across[step][:, inside : inside + step_dims])


def sums(parts, total, gram_a, gram_b):
    message = floats(1, total.shape[0] // parts + 128)
    return call(
        functools.partial(sums_kernel, parts, 1),
        "sums",
        [total, gram_a, gram_b],
        [message] * parts,
        [],
        10**9,
        16,
    )


def finish_kernel(*refs):
    messages, (features_ref, norm_ref) = refs[:-2], refs[-2:]
    part_dims = features_ref.shape[1]
    summed = messages[0][...]
    for message in messages[1:]:
        summed += message[...]
    sumsq = jnp.maximum(summed[:, part_dims : part_dims + 128], 0.0)
    scale = lax.rsqrt(sumsq + epsilon) * unscale
    for begin in range(0, part_dims, 128):
        width = min(128, part_dims - begin)
        features_ref[:, begin : begin + width] = summed[:, begin : begin + width] * scale[:, :width]
    norm_ref[0] = jnp.max(jnp.sqrt(sumsq))


def finish(messages, part_dims):
    return pl.pallas_call(
        finish_kernel,
        in_specs=[pl.BlockSpec(memory_space=pltpu.VMEM)] * len(messages),
        out_specs=[pl.BlockSpec(memory_space=space) for space in (pltpu.VMEM, pltpu.SMEM)],
        out_shape=[floats(1, part_dims), floats(1)],
        compiler_params=pltpu.CompilerParams(vmem_limit_bytes=4 * 2**20),
        name="finish",
    )(*messages)


def on_device(parts, group, activations, backprops, block_counters):
    tokens, columns = backprops.shape[1:]
    counters = block_counters.reshape(2)
    acts = activations[0]
    backs = backprops[0]
    if parts == 4 and group % 2 == 0:
        swap = [(0, 1), (1, 0), (2, 3), (3, 2)]
        halves = 2
        dims = K // halves

        def with_sibling(array):
            pairs = [(device, device ^ 1) for device in range(group)]
            return [array, lax.ppermute(array, "ex", pairs)]

        other_acts = lax.ppermute(with_digits(acts, counters), "param", swap)
        early_backs = lax.ppermute(backs, "param", [(0, 0), (1, 2), (2, 1), (3, 3)])
        own_pair = with_sibling(acts)
        late_backs = lax.ppermute(backs, "param", [(0, 2), (3, 1), (1, 0), (2, 3)])
        late_own, early_own = ahead(
            parts, halves, [("late", 0), ("early", 0)], [counters], columns, dims
        )
        u_own, gram_own = left(parts, halves, counters, own_pair, dims)
        other_acts, u_own, late_own, early_own = lax.optimization_barrier(
            (other_acts, u_own, late_own, early_own)
        )
        made = ahead(
            parts,
            halves,
            [("early", 0), ("late", 0), ("row", 0)],
            [other_acts],
            columns,
            dims,
        )
        u_other = partner_left(made[2], other_acts, tokens)
        other_acts, early_backs, late_backs, made, u_other = lax.optimization_barrier(
            (other_acts, early_backs, late_backs, made, u_other)
        )
        early_pair = with_sibling(early_backs)
        other_pair = with_sibling(other_acts)
        late_pair = with_sibling(late_backs)
        early_other, late_other, row_other = made
        cols = [early_own, early_other, late_own, late_other]
        messages = [None] * parts
        for which, other in enumerate((u_other, [row_other, other_pair[1]])):
            messages[which], messages[2 + which] = one_example(
                which,
                u_own,
                cols,
                other,
                early_pair[which],
                late_pair[which],
                gram_own,
                parts,
            )
        messages = lax.optimization_barrier(messages)
    else:
        halves = 1
        every_back = lax.all_gather(backs, "param", axis=1, tiled=True)
        u_own, gram_own = left(parts, halves, counters, [acts], K)
        total, gram_backs = middle(parts, halves, counters, [every_back], u_own)
        messages = sums(parts, total, gram_own, gram_backs)
    received = []
    for number, message in enumerate(messages):
        if halves == 1:
            moves = [(source, (source + number) % parts) for source in range(parts)]
            received.append(lax.ppermute(message, "param", moves) if number else message)
        else:
            moves = [
                (
                    z * group + chip * 2 + core,
                    (2 * (core ^ z // 2) + (z % 2 ^ number // 2)) * group
                    + chip * 2
                    + (core ^ number % 2),
                )
                for z in range(parts)
                for chip in range(group // 2)
                for core in range(2)
            ]
            received.append(lax.ppermute(message, ("param", "ex"), moves))
    features, norm = finish(received, K // parts)
    return (features, norm)


def solution(mesh):
    return jax.shard_map(
        functools.partial(on_device, mesh.shape["param"], mesh.shape["ex"]),
        mesh=mesh,
        in_specs=(
            P(("grp", "ex"), None, "param"),
            P(("grp", "ex"), None, "param"),
            P(None, "param"),
        ),
        out_specs=(P(("grp", "ex"), "param"), P(("grp", "ex"))),
        check_vma=False,
    )
```

```python
import functools

import jax
import jax.numpy as jnp
from jax import lax
from jax.experimental import pallas as pl
from jax.experimental.pallas import tpu as pltpu
from jax.sharding import PartitionSpec as P

K = 2048

mix_factor = 73244475
stream_factor = 668265261
row_factor = 374761393
col_factor = 1103515245
epsilon = 1e-06
unscale = 1.0 / (128.0 * 128.0)

tile = 256
sub_rows = 16
sub_cols = 256


def wrapped(number):
    return jnp.int32((number + 2**31) % 2**32 - 2**31)


def scramble(hashed):
    sixteen = jnp.int32(16)
    hashed = jnp.bitwise_xor(hashed, lax.shift_right_logical(hashed, sixteen))
    hashed = hashed * mix_factor
    hashed = jnp.bitwise_xor(hashed, lax.shift_right_logical(hashed, sixteen))
    hashed = hashed * mix_factor
    return jnp.bitwise_xor(hashed, lax.shift_right_logical(hashed, sixteen))


def to_gauss(hashed):
    hashed = scramble(hashed)
    pairs = jnp.int32(0x00FF00FF)
    two_sums = jnp.bitwise_and(hashed, pairs) + jnp.bitwise_and(
        lax.shift_right_logical(hashed, jnp.int32(8)), pairs
    )
    total = lax.shift_right_logical(two_sums * jnp.int32(0x10001), jnp.int32(16))
    return (total - 510).astype(jnp.float32).astype(jnp.bfloat16)


def fill_pattern(pattern_ref):
    shape = pattern_ref.shape
    pattern_ref[...] = (
        lax.broadcasted_iota(jnp.int32, shape, 0) * col_factor
        + lax.broadcasted_iota(jnp.int32, shape, 1) * row_factor
    )


def hash_rows(pattern_ref, out_ref, base, row, width):
    offset = base + (wrapped(row * col_factor) if isinstance(row, int) else row * col_factor)
    for first in range(0, width, sub_cols):
        last = min(first + sub_cols, width)
        out_ref[pl.ds(row, sub_rows), first:last] = to_gauss(pattern_ref[:, first:last] + offset)


def hash_tile(pattern_ref, out_ref, base):
    rows, width = out_ref.shape
    for row in range(0, rows, sub_rows):
        hash_rows(pattern_ref, out_ref, base, row, width)


def dot_nt(lhs, rhs):
    return lax.dot_general(
        lhs, rhs, (((1,), (1,)), ((), ())), preferred_element_type=jnp.float32
    )


def counter(source, which):
    if source.dtype == jnp.int32:
        return source[which]
    row = source[source.shape[0] - 16 :, 0:128].astype(jnp.float32)[0:1]
    lane = lax.broadcasted_iota(jnp.int32, row.shape, 1) - 3 * which
    zero = jnp.zeros_like(row)
    value = zero
    for digit in range(3):
        value += jnp.where(lane == digit, row * float(256**digit), zero)
    return jnp.sum(value).astype(jnp.int32)


def row_base(source, place, rows):
    return counter(source, 0) * stream_factor + place * wrapped(rows * row_factor)


def col_base(source, place, columns):
    return counter(source, 1) * stream_factor + place * wrapped(columns * row_factor)


def half():
    core = lax.rem(lax.axis_index("ex"), 2)
    return jnp.bitwise_xor(core, lax.shift_right_logical(lax.axis_index("param"), 1))


def first_dim(halves, dims):
    if halves == 1:
        return jnp.int32(0)
    return half() * wrapped(dims * col_factor)


def places(parts):
    place = lax.axis_index("param")
    if parts != 4:
        return place, place, jnp.int32(0), jnp.int32(0)
    early_at = 2 * jnp.bitwise_and(place, 1) + lax.shift_right_logical(place, 1)
    return place, jnp.bitwise_xor(place, 1), early_at, jnp.bitwise_xor(early_at, 1)


def rows_at(step, size):
    return pl.ds(pl.multiple_of(step * size, size), size)


def stream(steps, hash_at, use, beside_first):
    hash_at(0, 0)
    beside_first()

    def body(turn, carry):
        hash_at(2 * turn + 1, 1)
        use(2 * turn, 0)
        hash_at(2 * turn + 2, 0)
        use(2 * turn + 1, 1)
        return carry

    lax.fori_loop(0, steps // 2 - 1, body, 0)
    hash_at(steps - 1, 1)
    use(steps - 2, 0)
    use(steps - 1, 1)


def call(kernel, name, operands, outs, scratch, flops, megabytes):
    spaces = [pltpu.SMEM if array.dtype == jnp.int32 else pltpu.VMEM for array in operands]
    return pl.pallas_call(
        kernel,
        in_specs=[pl.BlockSpec(memory_space=space) for space in spaces],
        out_specs=[pl.BlockSpec(memory_space=pltpu.VMEM)] * len(outs),
        out_shape=outs,
        scratch_shapes=scratch,
        compiler_params=pltpu.CompilerParams(vmem_limit_bytes=megabytes * 2**20),
        cost_estimate=pl.CostEstimate(flops=flops, bytes_accessed=0, transcendentals=0),
        name=name,
    )(*operands)


def floats(*shape):
    return jax.ShapeDtypeStruct(shape, jnp.float32)


def digits_kernel(acts_ref, counters_ref, out_ref):
    tokens, rows = acts_ref.shape
    out_ref[:tokens, :] = acts_ref[...]
    lane = lax.broadcasted_iota(jnp.int32, (16, rows), 1)
    digits = jnp.zeros((16, rows), jnp.int32)
    for which in range(2):
        for digit in range(3):
            value = lax.shift_right_logical(counters_ref[which], jnp.int32(8 * digit))
            digits = jnp.where(lane == 3 * which + digit, jnp.bitwise_and(value, 255), digits)
    out_ref[tokens:, :] = digits.astype(jnp.float32).astype(out_ref.dtype)


def with_digits(acts, counters):
    tokens, rows = acts.shape
    (out,) = call(
        digits_kernel,
        "with_digits",
        [acts, counters],
        [jax.ShapeDtypeStruct((tokens + 16, rows), acts.dtype)],
        [],
        0,
        8,
    )
    return out


def ahead_kernel(parts, halves, kinds, sources, *refs):
    sources_in, outs, pattern_ref = refs[:sources], refs[sources:-1], refs[-1]
    _, partner, early_at, late_at = places(parts)
    dims, columns = outs[0].shape
    fill_pattern(pattern_ref)
    bases = []
    for kind, which in kinds:
        if kind == "row":
            base = row_base(sources_in[which], partner, columns)
        else:
            base = col_base(sources_in[which], early_at if kind == "early" else late_at, columns)
        bases.append(base + first_dim(halves, dims))

    def strip(number, carry):
        row = pl.multiple_of(number * sub_rows, sub_rows)
        for base, out_ref in zip(bases, outs):
            hash_rows(pattern_ref, out_ref, base, row, columns)
        return carry

    lax.fori_loop(0, dims // sub_rows, strip, 0, unroll=max(1, 4 // len(kinds)))


def ahead(parts, halves, kinds, sources, columns, dims):
    return call(
        functools.partial(ahead_kernel, parts, halves, kinds, len(sources)),
        "ahead",
        sources,
        [jax.ShapeDtypeStruct((dims, columns), jnp.bfloat16)] * len(kinds),
        [pltpu.VMEM((sub_rows, columns), jnp.int32)],
        1000 * dims * columns * len(kinds),
        8,
    )


def left_kernel(parts, halves, examples, source, *refs):
    acts = refs[:examples]
    u_ref, gram_ref, pattern_ref = refs[examples : examples + 3]
    tiles = refs[examples + 3 :]
    tokens, rows = acts[0].shape
    dims = u_ref.shape[0]
    fill_pattern(pattern_ref)
    base = row_base(source, places(parts)[0], rows) + first_dim(halves, dims)

    def hash_at(step, which):
        hash_tile(pattern_ref, tiles[which], base + step * wrapped(tile * col_factor))

    def grams():
        for e in range(examples):
            gram_ref[e] = dot_nt(acts[e][...], acts[e][...])

    def use(step, which):
        for e in range(examples):
            u_ref[rows_at(step, tile), e * tokens : (e + 1) * tokens] = dot_nt(
                tiles[which][...], acts[e][...]
            )

    stream(dims // tile, hash_at, use, grams)


def left(parts, halves, own, acts, dims):
    examples = len(acts)
    tokens, rows = acts[0].shape
    return call(
        functools.partial(left_kernel, parts, halves, examples),
        "left",
        [own, *acts],
        [floats(dims, examples * tokens), floats(examples, tokens, tokens)],
        [pltpu.VMEM((sub_rows, rows), jnp.int32)] + [pltpu.VMEM((tile, rows), jnp.bfloat16)] * 2,
        1000 * dims * rows,
        16,
    )


def middle_kernel(parts, halves, examples, source, u_ref, *refs):
    backs, refs = refs[:examples], refs[examples:]
    total_ref, gram_ref, pattern_ref = refs[:3]
    tiles = refs[3:]
    dims = total_ref.shape[0]
    tokens, columns = backs[0].shape
    fill_pattern(pattern_ref)
    base = col_base(source, places(parts)[2], columns) + first_dim(halves, dims)

    def hash_at(step, which):
        hash_tile(pattern_ref, tiles[which], base + step * wrapped(tile * col_factor))

    def grams():
        for e in range(examples):
            gram_ref[e] = dot_nt(backs[e][...], backs[e][...])

    def use(step, which):
        rows = rows_at(step, tile)
        for e in range(examples):
            here = slice(e * tokens, (e + 1) * tokens)
            total_ref[rows, here] = u_ref[rows, here] * dot_nt(tiles[which][...], backs[e][...])

    stream(dims // tile, hash_at, use, grams)


def middle(parts, halves, source, backs, u_own):
    examples = len(backs)
    tokens, columns = backs[0].shape
    dims = u_own.shape[0]
    return call(
        functools.partial(middle_kernel, parts, halves, examples),
        "middle",
        [source, u_own, *backs],
        [floats(dims, examples * tokens), floats(examples, tokens, tokens)],
        [pltpu.VMEM((sub_rows, columns), jnp.int32)]
        + [pltpu.VMEM((tile, columns), jnp.bfloat16)] * 2,
        1000 * dims * columns,
        20,
    )


def partner_kernel(row_other, acts, u_ref, gram_ref):
    tokens = u_ref.shape[1]
    for first in range(0, u_ref.shape[0], tile):
        rows = slice(first, first + tile)
        u_ref[rows, :] = dot_nt(row_other[rows, :], acts[:tokens, :])
    gram_ref[...] = dot_nt(acts[:tokens, :], acts[:tokens, :])


def partner_left(row_other, acts, tokens):
    dims = row_other.shape[0]
    return call(
        partner_kernel,
        "partner_left",
        [row_other, acts],
        [floats(dims, tokens), floats(tokens, tokens)],
        [],
        10**9,
        12,
    )


def example_kernel(which, *refs):
    u_own, early_own, early_other, late_own, late_other = refs[:5]
    first_other, second_other, early_backs, late_backs, gram_own = refs[5:10]
    outs = refs[10:]
    tokens = early_backs.shape[0]
    dims = early_own.shape[0]
    part_dims = outs[0].shape[1] - 128
    here = slice(which * tokens, (which + 1) * tokens)
    across = []
    for first in range(0, dims, tile):
        rows = slice(first, first + tile)
        right_own = dot_nt(early_own[rows, :], early_backs[...])
        right_own += dot_nt(late_own[rows, :], late_backs[...])
        right_other = dot_nt(early_other[rows, :], early_backs[...])
        right_other += dot_nt(late_other[rows, :], late_backs[...])
        if which:
            u_other = dot_nt(first_other[rows, :], second_other[:tokens, :])
        else:
            u_other = first_other[rows, :]
        total = u_own[rows, here] * right_own + u_other * right_other
        lane_sum = total[:, :128]
        for begin in range(128, tokens, 128):
            lane_sum += total[:, begin : begin + 128]
        across.append(jnp.sum(lane_sum.T, axis=0, keepdims=True))
    if which:
        gram_a = gram_own[which] + dot_nt(second_other[:tokens, :], second_other[:tokens, :])
    else:
        gram_a = gram_own[which] + second_other[...]
    gram_b = dot_nt(early_backs[...], early_backs[...]) + dot_nt(late_backs[...], late_backs[...])
    both = jnp.full((1, 128), jnp.sum(gram_a * gram_b), jnp.float32)
    low = jnp.bitwise_and(lax.axis_index("param"), 1)
    for number in range(len(outs)):
        slot = jnp.bitwise_xor(number, low)
        for at, out in enumerate(outs):

            @pl.when(slot == at)
            def _():
                out[:, part_dims:] = both
                for begin in range(0, part_dims, tile):
                    step = (number * part_dims + begin) // tile
                    out[:, begin : begin + tile] = across[step]


def one_example(which, u_own, cols, other, early_backs, late_backs, gram_own, parts):
    dims = cols[0].shape[0]
    return call(
        functools.partial(example_kernel, which),
        "one_example",
        [u_own, *cols, *other, early_backs, late_backs, gram_own],
        [floats(1, dims * 2 // parts + 128)] * 2,
        [],
        4 * 10**9,
        24,
    )


def sums_kernel(parts, examples, total_ref, gram_a_ref, gram_b_ref, *outs):
    tokens = gram_b_ref.shape[1]
    dims = total_ref.shape[0]
    part_dims = outs[0].shape[1] - 128
    place = lax.axis_index("param")

    def send(number, columns, values):
        slot = lax.rem(number - place + parts, parts)
        for which, out in enumerate(outs):

            @pl.when(slot == which)
            def _():
                out[:, columns] = values

    across = []
    for step in range(dims // tile):
        total = total_ref[step * tile : (step + 1) * tile, :]
        lane_sum = total[:, :128]
        for begin in range(128, tokens, 128):
            lane_sum += total[:, begin : begin + 128]
        across.append(jnp.sum(lane_sum.T, axis=0, keepdims=True))
    both = jnp.full((1, 128), jnp.sum(gram_a_ref[0] * gram_b_ref[0]), jnp.float32)
    step_dims = min(tile, part_dims)
    for number in range(parts):
        send(number, slice(part_dims, part_dims + 128), both)
        for begin in range(0, part_dims, step_dims):
            step, inside = divmod(number * part_dims + begin, tile)
            send(number, slice(begin, begin + step_dims), across[step][:, inside : inside + step_dims])


def sums(parts, total, gram_a, gram_b):
    message = floats(1, total.shape[0] // parts + 128)
    return call(
        functools.partial(sums_kernel, parts, 1),
        "sums",
        [total, gram_a, gram_b],
        [message] * parts,
        [],
        10**9,
        16,
    )


def finish_kernel(*refs):
    messages, (features_ref, norm_ref) = refs[:-2], refs[-2:]
    part_dims = features_ref.shape[1]
    summed = messages[0][...]
    for message in messages[1:]:
        summed += message[...]
    sumsq = jnp.maximum(summed[:, part_dims : part_dims + 128], 0.0)
    scale = lax.rsqrt(sumsq + epsilon) * unscale
    for begin in range(0, part_dims, 128):
        width = min(128, part_dims - begin)
        features_ref[:, begin : begin + width] = summed[:, begin : begin + width] * scale[:, :width]
    norm_ref[0] = jnp.max(jnp.sqrt(sumsq))


def finish(messages, part_dims):
    return pl.pallas_call(
        finish_kernel,
        in_specs=[pl.BlockSpec(memory_space=pltpu.VMEM)] * len(messages),
        out_specs=[pl.BlockSpec(memory_space=space) for space in (pltpu.VMEM, pltpu.SMEM)],
        out_shape=[floats(1, part_dims), floats(1)],
        compiler_params=pltpu.CompilerParams(vmem_limit_bytes=4 * 2**20),
        name="finish",
    )(*messages)


def on_device(parts, group, activations, backprops, block_counters):
    tokens, columns = backprops.shape[1:]
    counters = block_counters.reshape(2)
    acts = activations[0]
    backs = backprops[0]
    if parts == 4 and group % 2 == 0:
        swap = [(0, 1), (1, 0), (2, 3), (3, 2)]
        halves = 2
        dims = K // halves

        def with_sibling(array):
            pairs = [(device, device ^ 1) for device in range(group)]
            return [array, lax.ppermute(array, "ex", pairs)]

        payload, acts = lax.optimization_barrier((with_digits(acts, counters), acts))
        other_acts = lax.ppermute(payload, "param", swap)
        early_backs = lax.ppermute(backs, "param", [(0, 0), (1, 2), (2, 1), (3, 3)])
        own_pair = with_sibling(acts)
        late_backs = lax.ppermute(backs, "param", [(0, 2), (3, 1), (1, 0), (2, 3)])
        late_own, early_own = ahead(
            parts, halves, [("late", 0), ("early", 0)], [counters], columns, dims
        )
        u_own, gram_own = left(parts, halves, counters, own_pair, dims)
        other_acts, u_own, late_own, early_own = lax.optimization_barrier(
            (other_acts, u_own, late_own, early_own)
        )
        made = ahead(
            parts,
            halves,
            [("early", 0), ("late", 0), ("row", 0)],
            [other_acts],
            columns,
            dims,
        )
        u_other = partner_left(made[2], other_acts, tokens)
        other_acts, early_backs, late_backs, made, u_other = lax.optimization_barrier(
            (other_acts, early_backs, late_backs, made, u_other)
        )
        early_pair = with_sibling(early_backs)
        other_pair = with_sibling(other_acts)
        late_pair = with_sibling(late_backs)
        early_other, late_other, row_other = made
        cols = [early_own, early_other, late_own, late_other]
        messages = [None] * parts
        for which, other in enumerate((u_other, [row_other, other_pair[1]])):
            messages[which], messages[2 + which] = one_example(
                which,
                u_own,
                cols,
                other,
                early_pair[which],
                late_pair[which],
                gram_own,
                parts,
            )
        messages = lax.optimization_barrier(messages)
    else:
        halves = 1
        every_back = lax.all_gather(backs, "param", axis=1, tiled=True)
        u_own, gram_own = left(parts, halves, counters, [acts], K)
        total, gram_backs = middle(parts, halves, counters, [every_back], u_own)
        messages = sums(parts, total, gram_own, gram_backs)
    received = []
    for number, message in enumerate(messages):
        if halves == 1:
            moves = [(source, (source + number) % parts) for source in range(parts)]
            received.append(lax.ppermute(message, "param", moves) if number else message)
        else:
            moves = [
                (
                    z * group + chip * 2 + core,
                    (2 * (core ^ z // 2) + (z % 2 ^ number // 2)) * group
                    + chip * 2
                    + (core ^ number % 2),
                )
                for z in range(parts)
                for chip in range(group // 2)
                for core in range(2)
            ]
            received.append(lax.ppermute(message, ("param", "ex"), moves))
    features, norm = finish(received, K // parts)
    return (features, norm)


def solution(mesh):
    return jax.shard_map(
        functools.partial(on_device, mesh.shape["param"], mesh.shape["ex"]),
        mesh=mesh,
        in_specs=(
            P(("grp", "ex"), None, "param"),
            P(("grp", "ex"), None, "param"),
            P(None, "param"),
        ),
        out_specs=(P(("grp", "ex"), "param"), P(("grp", "ex"))),
        check_vma=False,
    )
```

```python
import functools

import jax
import jax.numpy as jnp
from jax import lax
from jax.experimental import pallas as pl
from jax.experimental.pallas import tpu as pltpu
from jax.sharding import PartitionSpec as P

K = 2048

mix_factor = 73244475
stream_factor = 668265261
row_factor = 374761393
col_factor = 1103515245
epsilon = 1e-06
unscale = 1.0 / (128.0 * 128.0)

tile = 256
sub_rows = 16
sub_cols = 256


def wrapped(number):
    return jnp.int32((number + 2**31) % 2**32 - 2**31)


def scramble(hashed):
    sixteen = jnp.int32(16)
    hashed = jnp.bitwise_xor(hashed, lax.shift_right_logical(hashed, sixteen))
    hashed = hashed * mix_factor
    hashed = jnp.bitwise_xor(hashed, lax.shift_right_logical(hashed, sixteen))
    hashed = hashed * mix_factor
    return jnp.bitwise_xor(hashed, lax.shift_right_logical(hashed, sixteen))


def to_gauss(hashed):
    hashed = scramble(hashed)
    pairs = jnp.int32(0x00FF00FF)
    two_sums = jnp.bitwise_and(hashed, pairs) + jnp.bitwise_and(
        lax.shift_right_logical(hashed, jnp.int32(8)), pairs
    )
    total = lax.shift_right_logical(two_sums * jnp.int32(0x10001), jnp.int32(16))
    return (total - 510).astype(jnp.float32).astype(jnp.bfloat16)


def fill_pattern(pattern_ref):
    shape = pattern_ref.shape
    pattern_ref[...] = (
        lax.broadcasted_iota(jnp.int32, shape, 0) * col_factor
        + lax.broadcasted_iota(jnp.int32, shape, 1) * row_factor
    )


def hash_rows(pattern_ref, out_ref, base, row, width):
    offset = base + (wrapped(row * col_factor) if isinstance(row, int) else row * col_factor)
    for first in range(0, width, sub_cols):
        last = min(first + sub_cols, width)
        out_ref[pl.ds(row, sub_rows), first:last] = to_gauss(pattern_ref[:, first:last] + offset)


def hash_tile(pattern_ref, out_ref, base):
    rows, width = out_ref.shape
    for row in range(0, rows, sub_rows):
        hash_rows(pattern_ref, out_ref, base, row, width)


def dot_nt(lhs, rhs):
    return lax.dot_general(
        lhs, rhs, (((1,), (1,)), ((), ())), preferred_element_type=jnp.float32
    )


def counter(source, which):
    if source.dtype == jnp.int32:
        return source[which]
    row = source[source.shape[0] - 16 :, 0:128].astype(jnp.float32)[0:1]
    lane = lax.broadcasted_iota(jnp.int32, row.shape, 1) - 3 * which
    zero = jnp.zeros_like(row)
    value = zero
    for digit in range(3):
        value += jnp.where(lane == digit, row * float(256**digit), zero)
    return jnp.sum(value).astype(jnp.int32)


def row_base(source, place, rows):
    return counter(source, 0) * stream_factor + place * wrapped(rows * row_factor)


def col_base(source, place, columns):
    return counter(source, 1) * stream_factor + place * wrapped(columns * row_factor)


def half():
    core = lax.rem(lax.axis_index("ex"), 2)
    return jnp.bitwise_xor(core, lax.shift_right_logical(lax.axis_index("param"), 1))


def first_dim(halves, dims):
    if halves == 1:
        return jnp.int32(0)
    return half() * wrapped(dims * col_factor)


def places(parts):
    place = lax.axis_index("param")
    if parts != 4:
        return place, place, jnp.int32(0), jnp.int32(0)
    early_at = 2 * jnp.bitwise_and(place, 1) + lax.shift_right_logical(place, 1)
    return place, jnp.bitwise_xor(place, 1), early_at, jnp.bitwise_xor(early_at, 1)


def rows_at(step, size):
    return pl.ds(pl.multiple_of(step * size, size), size)


def stream(steps, hash_at, use, beside_first):
    hash_at(0, 0)
    beside_first()

    def body(turn, carry):
        hash_at(2 * turn + 1, 1)
        use(2 * turn, 0)
        hash_at(2 * turn + 2, 0)
        use(2 * turn + 1, 1)
        return carry

    lax.fori_loop(0, steps // 2 - 1, body, 0)
    hash_at(steps - 1, 1)
    use(steps - 2, 0)
    use(steps - 1, 1)


def call(kernel, name, operands, outs, scratch, flops, megabytes):
    spaces = [pltpu.SMEM if array.dtype == jnp.int32 else pltpu.VMEM for array in operands]
    return pl.pallas_call(
        kernel,
        in_specs=[pl.BlockSpec(memory_space=space) for space in spaces],
        out_specs=[pl.BlockSpec(memory_space=pltpu.VMEM)] * len(outs),
        out_shape=outs,
        scratch_shapes=scratch,
        compiler_params=pltpu.CompilerParams(vmem_limit_bytes=megabytes * 2**20),
        cost_estimate=pl.CostEstimate(flops=flops, bytes_accessed=0, transcendentals=0),
        name=name,
    )(*operands)


def floats(*shape):
    return jax.ShapeDtypeStruct(shape, jnp.float32)


def digits_kernel(acts_ref, counters_ref, out_ref):
    tokens, rows = acts_ref.shape
    out_ref[:tokens, :] = acts_ref[...]
    lane = lax.broadcasted_iota(jnp.int32, (16, rows), 1)
    digits = jnp.zeros((16, rows), jnp.int32)
    for which in range(2):
        for digit in range(3):
            value = lax.shift_right_logical(counters_ref[which], jnp.int32(8 * digit))
            digits = jnp.where(lane == 3 * which + digit, jnp.bitwise_and(value, 255), digits)
    out_ref[tokens:, :] = digits.astype(jnp.float32).astype(out_ref.dtype)


def with_digits(acts, counters):
    tokens, rows = acts.shape
    (out,) = call(
        digits_kernel,
        "with_digits",
        [acts, counters],
        [jax.ShapeDtypeStruct((tokens + 16, rows), acts.dtype)],
        [],
        0,
        8,
    )
    return out


def ahead_kernel(parts, halves, kinds, sources, *refs):
    sources_in, outs, pattern_ref = refs[:sources], refs[sources:-1], refs[-1]
    _, partner, early_at, late_at = places(parts)
    dims, columns = outs[0].shape
    fill_pattern(pattern_ref)
    bases = []
    for kind, which in kinds:
        if kind == "row":
            base = row_base(sources_in[which], partner, columns)
        else:
            base = col_base(sources_in[which], early_at if kind == "early" else late_at, columns)
        bases.append(base + first_dim(halves, dims))

    def strip(number, carry):
        row = pl.multiple_of(number * sub_rows, sub_rows)
        for base, out_ref in zip(bases, outs):
            hash_rows(pattern_ref, out_ref, base, row, columns)
        return carry

    lax.fori_loop(0, dims // sub_rows, strip, 0, unroll=max(1, 4 // len(kinds)))


def ahead(parts, halves, kinds, sources, columns, dims):
    return call(
        functools.partial(ahead_kernel, parts, halves, kinds, len(sources)),
        "ahead",
        sources,
        [jax.ShapeDtypeStruct((dims, columns), jnp.bfloat16)] * len(kinds),
        [pltpu.VMEM((sub_rows, columns), jnp.int32)],
        1000 * dims * columns * len(kinds),
        8,
    )


def left_kernel(parts, halves, examples, source, *refs):
    acts = refs[:examples]
    u_ref, gram_ref, pattern_ref = refs[examples : examples + 3]
    tiles = refs[examples + 3 :]
    tokens, rows = acts[0].shape
    dims = u_ref.shape[0]
    fill_pattern(pattern_ref)
    base = row_base(source, places(parts)[0], rows) + first_dim(halves, dims)

    def hash_at(step, which):
        hash_tile(pattern_ref, tiles[which], base + step * wrapped(tile * col_factor))

    def grams():
        for e in range(examples):
            gram_ref[e] = dot_nt(acts[e][...], acts[e][...])

    def use(step, which):
        for e in range(examples):
            u_ref[rows_at(step, tile), e * tokens : (e + 1) * tokens] = dot_nt(
                tiles[which][...], acts[e][...]
            )

    stream(dims // tile, hash_at, use, grams)


def left(parts, halves, own, acts, dims):
    examples = len(acts)
    tokens, rows = acts[0].shape
    return call(
        functools.partial(left_kernel, parts, halves, examples),
        "left",
        [own, *acts],
        [floats(dims, examples * tokens), floats(examples, tokens, tokens)],
        [pltpu.VMEM((sub_rows, rows), jnp.int32)] + [pltpu.VMEM((tile, rows), jnp.bfloat16)] * 2,
        1000 * dims * rows,
        16,
    )


def middle_kernel(parts, halves, examples, source, u_ref, *refs):
    backs, refs = refs[:examples], refs[examples:]
    total_ref, gram_ref, pattern_ref = refs[:3]
    tiles = refs[3:]
    dims = total_ref.shape[0]
    tokens, columns = backs[0].shape
    fill_pattern(pattern_ref)
    base = col_base(source, places(parts)[2], columns) + first_dim(halves, dims)

    def hash_at(step, which):
        hash_tile(pattern_ref, tiles[which], base + step * wrapped(tile * col_factor))

    def grams():
        for e in range(examples):
            gram_ref[e] = dot_nt(backs[e][...], backs[e][...])

    def use(step, which):
        rows = rows_at(step, tile)
        for e in range(examples):
            here = slice(e * tokens, (e + 1) * tokens)
            total_ref[rows, here] = u_ref[rows, here] * dot_nt(tiles[which][...], backs[e][...])

    stream(dims // tile, hash_at, use, grams)


def middle(parts, halves, source, backs, u_own):
    examples = len(backs)
    tokens, columns = backs[0].shape
    dims = u_own.shape[0]
    return call(
        functools.partial(middle_kernel, parts, halves, examples),
        "middle",
        [source, u_own, *backs],
        [floats(dims, examples * tokens), floats(examples, tokens, tokens)],
        [pltpu.VMEM((sub_rows, columns), jnp.int32)]
        + [pltpu.VMEM((tile, columns), jnp.bfloat16)] * 2,
        1000 * dims * columns,
        20,
    )


def partner_kernel(row_other, acts, u_ref, gram_ref):
    tokens = u_ref.shape[1]
    for first in range(0, u_ref.shape[0], tile):
        rows = slice(first, first + tile)
        u_ref[rows, :] = dot_nt(row_other[rows, :], acts[:tokens, :])
    gram_ref[...] = dot_nt(acts[:tokens, :], acts[:tokens, :])


def partner_left(row_other, acts, tokens):
    dims = row_other.shape[0]
    return call(
        partner_kernel,
        "partner_left",
        [row_other, acts],
        [floats(dims, tokens), floats(tokens, tokens)],
        [],
        10**9,
        12,
    )


def example_kernel(which, *refs):
    u_own, early_own, early_other, late_own, late_other = refs[:5]
    first_other, second_other, early_backs, late_backs, gram_own = refs[5:10]
    outs = refs[10:]
    tokens = early_backs.shape[0]
    dims = early_own.shape[0]
    part_dims = outs[0].shape[1] - 128
    here = slice(which * tokens, (which + 1) * tokens)
    across = []
    for first in range(0, dims, tile):
        rows = slice(first, first + tile)
        right_own = dot_nt(early_own[rows, :], early_backs[...])
        right_own += dot_nt(late_own[rows, :], late_backs[...])
        right_other = dot_nt(early_other[rows, :], early_backs[...])
        right_other += dot_nt(late_other[rows, :], late_backs[...])
        if which:
            u_other = dot_nt(first_other[rows, :], second_other[:tokens, :])
        else:
            u_other = first_other[rows, :]
        total = u_own[rows, here] * right_own + u_other * right_other
        lane_sum = total[:, :128]
        for begin in range(128, tokens, 128):
            lane_sum += total[:, begin : begin + 128]
        across.append(jnp.sum(lane_sum.T, axis=0, keepdims=True))
    if which:
        gram_a = gram_own[which] + dot_nt(second_other[:tokens, :], second_other[:tokens, :])
    else:
        gram_a = gram_own[which] + second_other[...]
    gram_b = dot_nt(early_backs[...], early_backs[...]) + dot_nt(late_backs[...], late_backs[...])
    both = jnp.full((1, 128), jnp.sum(gram_a * gram_b), jnp.float32)
    low = jnp.bitwise_and(lax.axis_index("param"), 1)
    for number in range(len(outs)):
        slot = jnp.bitwise_xor(number, low)
        for at, out in enumerate(outs):

            @pl.when(slot == at)
            def _():
                out[:, part_dims:] = both
                for begin in range(0, part_dims, tile):
                    step = (number * part_dims + begin) // tile
                    out[:, begin : begin + tile] = across[step]


def one_example(which, u_own, cols, other, early_backs, late_backs, gram_own, parts):
    dims = cols[0].shape[0]
    return call(
        functools.partial(example_kernel, which),
        "one_example",
        [u_own, *cols, *other, early_backs, late_backs, gram_own],
        [floats(1, dims * 2 // parts + 128)] * 2,
        [],
        4 * 10**9,
        24,
    )


def sums_kernel(parts, examples, total_ref, gram_a_ref, gram_b_ref, *outs):
    tokens = gram_b_ref.shape[1]
    dims = total_ref.shape[0]
    part_dims = outs[0].shape[1] - 128
    place = lax.axis_index("param")

    def send(number, columns, values):
        slot = lax.rem(number - place + parts, parts)
        for which, out in enumerate(outs):

            @pl.when(slot == which)
            def _():
                out[:, columns] = values

    across = []
    for step in range(dims // tile):
        total = total_ref[step * tile : (step + 1) * tile, :]
        lane_sum = total[:, :128]
        for begin in range(128, tokens, 128):
            lane_sum += total[:, begin : begin + 128]
        across.append(jnp.sum(lane_sum.T, axis=0, keepdims=True))
    both = jnp.full((1, 128), jnp.sum(gram_a_ref[0] * gram_b_ref[0]), jnp.float32)
    step_dims = min(tile, part_dims)
    for number in range(parts):
        send(number, slice(part_dims, part_dims + 128), both)
        for begin in range(0, part_dims, step_dims):
            step, inside = divmod(number * part_dims + begin, tile)
            send(number, slice(begin, begin + step_dims), across[step][:, inside : inside + step_dims])


def sums(parts, total, gram_a, gram_b):
    message = floats(1, total.shape[0] // parts + 128)
    return call(
        functools.partial(sums_kernel, parts, 1),
        "sums",
        [total, gram_a, gram_b],
        [message] * parts,
        [],
        10**9,
        16,
    )


def finish_kernel(*refs):
    messages, (features_ref, norm_ref) = refs[:-2], refs[-2:]
    part_dims = features_ref.shape[1]
    summed = messages[0][...]
    for message in messages[1:]:
        summed += message[...]
    sumsq = jnp.maximum(summed[:, part_dims : part_dims + 128], 0.0)
    scale = lax.rsqrt(sumsq + epsilon) * unscale
    for begin in range(0, part_dims, 128):
        width = min(128, part_dims - begin)
        features_ref[:, begin : begin + width] = summed[:, begin : begin + width] * scale[:, :width]
    norm_ref[0] = jnp.max(jnp.sqrt(sumsq))


def finish(messages, part_dims):
    return pl.pallas_call(
        finish_kernel,
        in_specs=[pl.BlockSpec(memory_space=pltpu.VMEM)] * len(messages),
        out_specs=[pl.BlockSpec(memory_space=space) for space in (pltpu.VMEM, pltpu.SMEM)],
        out_shape=[floats(1, part_dims), floats(1)],
        compiler_params=pltpu.CompilerParams(vmem_limit_bytes=4 * 2**20),
        name="finish",
    )(*messages)


def on_device(parts, group, activations, backprops, block_counters):
    tokens, columns = backprops.shape[1:]
    counters = block_counters.reshape(2)
    acts = activations[0]
    backs = backprops[0]
    if parts == 4 and group % 2 == 0:
        swap = [(0, 1), (1, 0), (2, 3), (3, 2)]
        halves = 2
        dims = K // halves

        def with_sibling(array):
            pairs = [(device, device ^ 1) for device in range(group)]
            return [array, lax.ppermute(array, "ex", pairs)]

        payload, acts = lax.optimization_barrier((with_digits(acts, counters), acts))
        other_acts = lax.ppermute(payload, "param", swap)
        early_backs = lax.ppermute(backs, "param", [(0, 0), (1, 2), (2, 1), (3, 3)])
        own_pair = with_sibling(acts)
        late_backs = lax.ppermute(backs, "param", [(0, 2), (3, 1), (1, 0), (2, 3)])
        late_own, early_own = ahead(
            parts, halves, [("late", 0), ("early", 0)], [counters], columns, dims
        )
        u_own, gram_own = left(parts, halves, counters, own_pair, dims)
        other_acts, u_own, late_own, early_own = lax.optimization_barrier(
            (other_acts, u_own, late_own, early_own)
        )
        made = ahead(
            parts,
            halves,
            [("early", 0), ("late", 0), ("row", 0)],
            [other_acts],
            columns,
            dims,
        )
        u_other = partner_left(made[2], other_acts, tokens)
        other_acts, made = lax.optimization_barrier((other_acts, made))
        other_pair = with_sibling(other_acts)
        u_other = partner_left(made[2], other_acts, tokens)
        early_backs, late_backs, u_other = lax.optimization_barrier(
            (early_backs, late_backs, u_other)
        )
        early_pair = with_sibling(early_backs)
        late_pair = with_sibling(late_backs)
        early_other, late_other, row_other = made
        cols = [early_own, early_other, late_own, late_other]
        messages = [None] * parts
        for which, other in enumerate((u_other, [row_other, other_pair[1]])):
            messages[which], messages[2 + which] = one_example(
                which,
                u_own,
                cols,
                other,
                early_pair[which],
                late_pair[which],
                gram_own,
                parts,
            )
        messages = lax.optimization_barrier(messages)
    else:
        halves = 1
        every_back = lax.all_gather(backs, "param", axis=1, tiled=True)
        u_own, gram_own = left(parts, halves, counters, [acts], K)
        total, gram_backs = middle(parts, halves, counters, [every_back], u_own)
        messages = sums(parts, total, gram_own, gram_backs)
    received = []
    for number, message in enumerate(messages):
        if halves == 1:
            moves = [(source, (source + number) % parts) for source in range(parts)]
            received.append(lax.ppermute(message, "param", moves) if number else message)
        else:
            moves = [
                (
                    z * group + chip * 2 + core,
                    (2 * (core ^ z // 2) + (z % 2 ^ number // 2)) * group
                    + chip * 2
                    + (core ^ number % 2),
                )
                for z in range(parts)
                for chip in range(group // 2)
                for core in range(2)
            ]
            received.append(lax.ppermute(message, ("param", "ex"), moves))
    features, norm = finish(received, K // parts)
    return (features, norm)


def solution(mesh):
    return jax.shard_map(
        functools.partial(on_device, mesh.shape["param"], mesh.shape["ex"]),
        mesh=mesh,
        in_specs=(
            P(("grp", "ex"), None, "param"),
            P(("grp", "ex"), None, "param"),
            P(None, "param"),
        ),
        out_specs=(P(("grp", "ex"), "param"), P(("grp", "ex"))),
        check_vma=False,
    )
```
